256 devices in a mesh: dp: 32 (over x, y, core), mp: 8 (over z).
Axes of the slice: x: 4, y: 4, z: 8, core: 2. Of those that a mesh axis runs over, the one named last changes fastest.
Arguments:
- grad_down: bfloat16 [32, 4096, 5120], P('dp', None, 'mp'), may hold values from -6 to 6
- grad_out: bfloat16 [32, 4096, 5120], P('dp', None, 'mp'), may hold values from -6 to 6
- momentum_down: float32 [4096, 5120], P('dp', 'mp'), as said below
- momentum_out: float32 [4096, 5120], P('dp', 'mp'), as said below
- master_down: float32 [4096, 5120], P('dp', 'mp'), may hold values from -6 to 6
- master_out: float32 [4096, 5120], P('dp', 'mp'), may hold values from -6 to 6
Outputs:
- new_momentum_down: float32 [4096, 5120], P('dp', 'mp')
- new_momentum_out: float32 [4096, 5120], P('dp', 'mp')
- weights_down: bfloat16 [4096, 5120], P(None, 'mp')
- weights_out: bfloat16 [4096, 5120], P(None, 'mp')
The draws below stay inside these ranges and needn't reach their ends.
Inputs may be any that keep to these rules, and one draw needn't show every extreme that they name: `momentum_down`: real-valued momentum entries. `momentum_out`: real-valued momentum entries.
All inputs are finite; a program needn't handle non-finite values.
Results may differ from the reference program's by a relative error of at most 0.0004.
Values may be sent and summed in bfloat16 or wider, within the bound.
A program may use at most 128 MiB of HBM per device.

```python
import math
import jax
import jax.numpy as jnp
from jax import lax

D = 5120
BLK = 128
ITERS = 3
ROWS = 4096
N_DP = 32


def scaled_rows(key, top):
    key_base, key_row, key_col = jax.random.split(key, 3)
    base = jax.random.truncated_normal(key_base, -3.0, 3.0, (ROWS, D), jnp.float32)
    row_scale = jnp.exp(jax.random.uniform(key_row, (ROWS,), jnp.float32, 0.0, math.log(3.0)))
    rough = jnp.exp(jax.random.uniform(key_col, (D,), jnp.float32, 0.0, math.log(2.0)))
    place = jnp.arange(D, dtype=jnp.float32) / (D - 1)
    rise = jnp.exp(place * math.log(top))
    return base * row_scale[:, None] * (rise * rough)[None, :]


def draw_momentum_down(key, part):
    key = jax.random.fold_in(key, 11)
    return scaled_rows(key, 10.0)


def draw_momentum_out(key, part):
    key = jax.random.fold_in(key, 23)
    return scaled_rows(key, 10.0)


def raised(array, stream_key, source, target, shards_of, factor):
    owner, partner = [(jnp.arange(array.shape[axis_at]) // (array.shape[axis_at] // shards_of)).reshape([-1 if axis == axis_at else 1 for axis in range(array.ndim)]) for axis_at in (source, target)]
    chosen = jax.random.permutation(stream_key, shards_of)[partner]
    strong = (owner == chosen) | (owner == (partner + shards_of // 2) % shards_of)
    return jnp.where(strong, factor * array, array)


def level_of(rng, shape, shards, low, top_value):
    loudness = 1.0
    for position, shards_of in shards:
        steps = jax.random.uniform(jax.random.fold_in(jax.random.fold_in(rng, 6), position), (shards_of,), jnp.float32, low / len(shards), top_value / len(shards))
        loudness = loudness * jnp.repeat(jnp.exp(steps), shape[position] // shards_of).reshape((-1,) + (1,) * (len(shape) - 1 - position))
    return loudness


def scatter_about(stream_key, dims, width, reach, pieces=(), kind=jnp.bfloat16):
    entries = width * jax.random.normal(stream_key, dims, jnp.float32)
    if pieces:
        entries = entries * level_of(stream_key, dims, pieces, -0.22, 0.18)
    return jnp.clip(entries, -reach, reach).astype(kind)


def noise_with(key, extent, deviation, bound, cuts, heavy, kind=jnp.bfloat16):
    drawn = deviation * jax.random.normal(key, extent, jnp.float32)
    if cuts:
        drawn = drawn * level_of(key, extent, cuts, -0.22, 0.18)
    return jnp.clip(raised(drawn, jax.random.fold_in(key, 3), *heavy), -bound, bound).astype(kind)


def setup_inputs(seed: int = 0) -> dict:
    splits = jax.random.split(jax.random.key(seed), 7)
    return {
        "grad_down": noise_with(splits[0], (N_DP, ROWS, D), 1.0, 6.0, ((0, 32), (2, 8)), (0, 1, 32, 2.75)),
        "grad_out": noise_with(splits[1], (N_DP, ROWS, D), 1.0, 6.0, ((0, 32), (2, 8)), (0, 1, 32, 2.75)),
        "momentum_down": draw_momentum_down(jax.random.fold_in(splits[6], 71), 0),
        "momentum_out": draw_momentum_out(jax.random.fold_in(splits[6], 71), 0),
        "master_down": scatter_about(splits[4], (ROWS, D), 1.0, 6.0, ((0, 32), (1, 8)), jnp.float32),
        "master_out": scatter_about(splits[5], (ROWS, D), 1.0, 6.0, ((0, 32), (1, 8)), jnp.float32),
    }


momentum_coef = 0.95
learn_rate = 0.5
decay_rate = 0.1
coef_a = 3.4445
coef_b = -4.775
coef_c = 2.0315
norm_eps = 1e-07

def orthogonalize(block):
    x = block / (jnp.sqrt(jnp.sum(block * block)) + norm_eps)
    for step in range(ITERS):
        gram = jnp.dot(x, x.T, precision=lax.Precision.HIGHEST, preferred_element_type=jnp.float32)
        poly = coef_b * gram + coef_c * jnp.dot(gram, gram, precision=lax.Precision.HIGHEST, preferred_element_type=jnp.float32)
        x = coef_a * x + jnp.dot(poly, x, precision=lax.Precision.HIGHEST, preferred_element_type=jnp.float32)
    return x

def update_matrix(grad, momentum, master):

    def add_one(index, acc):
        return acc + grad[index].astype(jnp.float32)
    total = lax.fori_loop(0, grad.shape[0], add_one, jnp.zeros(grad.shape[1:], jnp.float32))
    new_momentum = momentum_coef * momentum + total
    look = total + momentum_coef * new_momentum
    blocks = look.reshape(N_DP, BLK, D)
    ortho = lax.map(orthogonalize, blocks).reshape(ROWS, D)
    weights = (1.0 - learn_rate * decay_rate) * master - learn_rate * 0.2 * math.sqrt(D) * ortho
    return (new_momentum, weights.astype(jnp.bfloat16))

def reference(grad_down, grad_out, momentum_down, momentum_out, master_down, master_out):
    mom_down, new_down = update_matrix(grad_down, momentum_down, master_down)
    mom_out, new_out = update_matrix(grad_out, momentum_out, master_out)
    return (mom_down, mom_out, new_down, new_out)
```

```python
import functools
import math

import jax
import jax.numpy as jnp
from jax import lax
from jax.experimental import pallas as pl
from jax.experimental.pallas import tpu as pltpu
from jax.sharding import PartitionSpec as P

D = 5120
BLK = 128
ITERS = 3
NX, NY, NC = 4, 4, 2
HALF = 64
QUART = 32
MESH = pl.DeviceIdType.MESH

momentum_coef = 0.95
learn_rate = 0.5
decay_rate = 0.1
coef_a = 3.4445
coef_b = -4.775
coef_c = 2.0315
norm_eps = 1e-07

WIRE = jnp.float32


def encode(x):
    return x


def decode(y):
    return y


def dot(a, b):
    return jnp.dot(a, b, precision=lax.Precision.HIGHEST, preferred_element_type=jnp.float32)


def kernel(
    nz, width,
    grad_down, grad_out, mom_down, mom_out, mas_down, mas_out,
    new_down, new_out, out_down, out_out,
    own, sib, s2, r2, s1, r1, acc, rr2, rr1, mom, mas, look, gpart, gslot, gfull,
    small_sem, own_sem, sib_ss, sib_rs,
    p1_ss, p1_rs, p2_ss, p2_rs,
    ga_ss, ga_rs, gb_ss, gb_rs,
    aa_ss, aa_rs, ab_ss, ab_rs, as_ss, as_rs,
):
    grads, moms, mass = (grad_down, grad_out), (mom_down, mom_out), (mas_down, mas_out)
    news, outs = (new_down, new_out), (out_down, out_out)
    dp, z = lax.axis_index("dp"), lax.axis_index("mp")
    c = lax.rem(dp, 2)
    chip = lax.div(dp, 2)
    y = lax.rem(chip, NY)
    x = lax.div(chip, NY)
    other = 1 - c

    def wrap(v):
        return lax.rem(v + 4, 4)

    def device(px, py, pc=c, pz=z):
        return ((px * NY + py) * NC + pc, pz)

    sibling = device(x, y, other)
    pos = ((x, y), (y, x))

    def along(h, axis, step):
        use_x = (axis == 0) == (h == 0)
        return device(wrap(x + step), y) if use_x else device(x, wrap(y + step))

    def chip_at(h, a, b):
        return (a, b) if h == 0 else (b, a)

    def remote(src, dst, ss, rs, dev):
        return pltpu.make_async_remote_copy(
            src_ref=src, dst_ref=dst, send_sem=ss, recv_sem=rs, device_id=dev, device_id_type=MESH
        )

    sends = []

    def send(src, dst, ss, rs, dev):
        copy = remote(src, dst, ss, rs, dev)
        copy.start()
        sends.append(copy)

    def landed(dst, rs):
        pltpu.make_async_copy(dst, dst, rs).wait()

    order = (2, 1, 3, 0)

    def source(m, h, da, core):
        a = wrap(pos[h][0] + da)
        if h == 0:
            return grads[m].at[a, :, core, 0:HALF, :]
        return grads[m].at[:, a, core, HALF:BLK, :]

    own_copies = {}
    for m in range(2):
        for da in order:
            for h in range(2):
                mh = 2 * m + h
                copy = pltpu.make_async_copy(source(m, h, da, c), own.at[mh, da], own_sem.at[mh, da])
                copy.start()
                own_copies[mh, da] = copy
    small = []
    for m in range(2):
        for k, (src, dst) in enumerate(((moms[m], mom.at[m]), (mass[m], mas.at[m]))):
            copy = pltpu.make_async_copy(src, dst, small_sem.at[m, k])
            copy.start()
            small.append(copy)

    barrier = pltpu.get_barrier_semaphore()
    peers = [sibling]
    for h in range(2):
        peers += [along(h, 0, 1), along(h, 0, -1)]
    peers += [device(x, y, c, lax.rem(z + k, nz)) for k in range(1, nz)]
    for peer in peers:
        pl.semaphore_signal(barrier, inc=1, device_id=peer, device_id_type=MESH)
    pl.semaphore_wait(barrier, len(peers))

    for m in range(2):
        for da in order:
            for h in range(2):
                mh = 2 * m + h
                send(source(m, h, da, other), sib.at[mh, da], sib_ss.at[mh, da], sib_rs.at[mh, da], sibling)

    def have(m, da):
        for h in range(2):
            own_copies[2 * m + h, da].wait()
            landed(sib.at[2 * m + h, da], sib_rs.at[2 * m + h, da])

    def pair(mh, da, b, lo):
        rows = pl.ds(lo, QUART)
        return own[mh, da, b, rows, :].astype(jnp.float32) + sib[mh, da, b, rows, :].astype(jnp.float32)

    def p1_far(m):
        have(m, 2)
        for h in range(2):
            mh = 2 * m + h
            for d in range(2):
                @pl.loop(0, 4)
                def _(b):
                    s2[mh, d, b] = encode(pair(mh, 2, b, QUART * d))
                send(s2.at[mh, d], r2.at[mh, d], p1_ss.at[mh, d, 0], p1_rs.at[mh, d, 0], along(h, 0, 1 - 2 * d))

    def p1_early(m):
        have(m, 1)
        have(m, 3)
        for h in range(2):
            mh = 2 * m + h
            for d in range(2):
                @pl.loop(0, 4)
                def _(b):
                    s1[mh, d, 0, b] = encode(pair(mh, 1 + 2 * d, b, QUART * (1 - d)))
                send(s1.at[mh, d, 0], r1.at[mh, d, 0], p1_ss.at[mh, d, 1], p1_rs.at[mh, d, 1], along(h, 0, 1 - 2 * d))

    def p1_late(m):
        for h in range(2):
            mh = 2 * m + h
            for d in range(2):
                landed(r2.at[mh, d], p1_rs.at[mh, d, 0])

                @pl.loop(0, 4)
                def _(b):
                    s1[mh, d, 1, b] = encode(pair(mh, 1 + 2 * d, b, QUART * d) + decode(r2[mh, d, b]))
                send(s1.at[mh, d, 1], r1.at[mh, d, 1], p1_ss.at[mh, d, 2], p1_rs.at[mh, d, 2], along(h, 0, 1 - 2 * d))

    def p1_end(m):
        have(m, 0)
        for h in range(2):
            mh = 2 * m + h
            for d in range(2):
                for e in range(2):
                    landed(r1.at[mh, d, e], p1_rs.at[mh, d, 1 + e])

            @pl.loop(0, 4)
            def _(b):
                for q in range(2):
                    acc[mh, b, pl.ds(QUART * q, QUART), :] = (
                        pair(mh, 0, b, QUART * q) + decode(r1[mh, q, 1, b]) + decode(r1[mh, 1 - q, 0, b])
                    )

    def p2_first(m):
        for h in range(2):
            mh = 2 * m + h
            at = pos[h][1]
            for d in range(2):
                to = along(h, 1, 1 - 2 * d)
                far = acc.at[mh, wrap(at + 2), pl.ds(QUART * d, QUART), :]
                send(far, rr2.at[mh, d], p2_ss.at[mh, d, 0], p2_rs.at[mh, d, 0], to)
            for d in range(2):
                to = along(h, 1, 1 - 2 * d)
                near = acc.at[mh, wrap(at + 1 - 2 * d), pl.ds(QUART * (1 - d), QUART), :]
                send(near, rr1.at[mh, d, 0], p2_ss.at[mh, d, 1], p2_rs.at[mh, d, 1], to)

    def p2_late(m):
        for h in range(2):
            mh = 2 * m + h
            for d in range(2):
                landed(rr2.at[mh, d], p2_rs.at[mh, d, 0])
                near = acc.at[mh, wrap(pos[h][1] + 1 - 2 * d), pl.ds(QUART * d, QUART), :]
                near[...] = near[...] + rr2[mh, d]
                send(near, rr1.at[mh, d, 1], p2_ss.at[mh, d, 2], p2_rs.at[mh, d, 2], along(h, 1, 1 - 2 * d))

    def p2_end(m):
        if m == 0:
            for copy in small:
                copy.wait()
        for h in range(2):
            mh = 2 * m + h
            for d in range(2):
                for e in range(2):
                    landed(rr1.at[mh, d, e], p2_rs.at[mh, d, 1 + e])
            for q in range(2):
                rows = pl.ds(HALF * h + QUART * q, QUART)
                total = acc[mh, pos[h][1], pl.ds(QUART * q, QUART), :] + rr1[mh, q, 1] + rr1[mh, 1 - q, 0]
                new = momentum_coef * mom[m, rows, :] + total
                news[m][rows, :] = new
                look[m, rows, :] = total + momentum_coef * new
        u = look[m]
        gram = lax.dot_general(
            u, u, (((1,), (1,)), ((), ())),
            precision=lax.Precision.HIGHEST, preferred_element_type=jnp.float32,
        )
        gpart[m] = gram.reshape(nz, BLK // nz, BLK)
        for k in range(1, nz):
            to = lax.rem(z + k, nz)
            send(gpart.at[m, to], gslot.at[m, k - 1], ga_ss.at[m, k - 1], ga_rs.at[m], device(x, y, c, to))

    def gram_sum(m):
        landed(gslot.at[m], ga_rs.at[m])
        total = gpart[m, z]
        for k in range(nz - 1):
            total = total + gslot[m, k]
        gfull[m, z] = total
        for k in range(1, nz):
            to = lax.rem(z + k, nz)
            send(gfull.at[m, z], gfull.at[m, z], gb_ss.at[m, k - 1], gb_rs.at[m], device(x, y, c, to))

    def update(m):
        landed(gslot.at[m], gb_rs.at[m])
        gram = gfull[m].reshape(BLK, BLK)
        eye = lax.broadcasted_iota(jnp.int32, (BLK, BLK), 0) == lax.broadcasted_iota(jnp.int32, (BLK, BLK), 1)
        diag = jnp.where(eye, gram, 0.0)
        square = jnp.sum(jnp.sum(diag, axis=1, keepdims=True), axis=0, keepdims=True)
        inv = 1.0 / (jnp.sqrt(square) + norm_eps)
        gram = gram * inv * inv
        ident = jnp.where(eye, coef_a, 0.0)
        whole = None
        for step in range(ITERS):
            factor = ident + coef_b * gram + coef_c * dot(gram, gram)
            whole = factor if whole is None else dot(factor, whole)
            if step < ITERS - 1:
                gram = dot(dot(factor, gram), factor)
        ortho = dot(whole * inv, look[m])
        scale = learn_rate * 0.2 * math.sqrt(D)
        weights = (1.0 - learn_rate * decay_rate) * mas[m] - scale * ortho
        outs[m][x, y, c] = weights.astype(jnp.bfloat16)

    def block(m, h, a, b, lo=0, n=HALF):
        px, py = chip_at(h, a, b)
        return outs[m].at[px, py, c, pl.ds(HALF * h + lo, n), :]

    def hand(m, h, k, a, b):
        ref = block(m, h, a, b)
        send(ref, ref, as_ss.at[2 * m + h, k], as_rs.at[m], sibling)

    def fan(m, h, j, a):
        mh, ref = 2 * m + h, block(m, h, a, pos[h][1])
        for d in range(2):
            send(ref, ref, ab_ss.at[mh, j, d], ab_rs.at[mh, j, d], along(h, 1, 1 - 2 * d))

    def cols(h):
        a = pos[h][0]
        return (a, wrap(a - 1), wrap(a + 1), wrap(a + 2))

    def g_start(m):
        for h in range(2):
            mh, (a, b) = 2 * m + h, pos[h]
            ref = block(m, h, a, b)
            for d in range(2):
                send(ref, ref, aa_ss.at[mh, d], aa_rs.at[mh, d], along(h, 0, 1 - 2 * d))
        for h in range(2):
            fan(m, h, 0, pos[h][0])
            hand(m, h, 0, *pos[h])

    def g_first(m):
        for h in range(2):
            mh, (a, b) = 2 * m + h, pos[h]
            for d in range(2):
                col = cols(h)[1 + d]
                ref = block(m, h, col, b)
                landed(ref, aa_rs.at[mh, d])
                part = block(m, h, col, b, QUART * d, QUART)
                send(part, part, aa_ss.at[mh, 2 + d], aa_rs.at[mh, 2 + d], along(h, 0, 1 - 2 * d))
                fan(m, h, 1 + d, col)
                hand(m, h, 1 + d, col, b)

    def g_far(m):
        for h in range(2):
            mh, (a, b) = 2 * m + h, pos[h]
            col = cols(h)[3]
            for d in range(2):
                landed(block(m, h, col, b, QUART * d, QUART), aa_rs.at[mh, 2 + d])
            fan(m, h, 3, col)
            hand(m, h, 3, col, b)

    def g_pass(m, j):
        for h in range(2):
            mh, b = 2 * m + h, pos[h][1]
            col = cols(h)[j]
            for d in range(2):
                row = wrap(b - 1 + 2 * d)
                landed(block(m, h, col, row), ab_rs.at[mh, j, d])
                part = block(m, h, col, row, QUART * d, QUART)
                send(part, part, ab_ss.at[mh, j, 2 + d], ab_rs.at[mh, j, 2 + d], along(h, 1, 1 - 2 * d))
                hand(m, h, 4 + 3 * j + d, col, row)

    def g_last(m, j):
        for h in range(2):
            mh, b = 2 * m + h, pos[h][1]
            col, row = cols(h)[j], wrap(b + 2)
            for d in range(2):
                landed(block(m, h, col, row, QUART * d, QUART), ab_rs.at[mh, j, 2 + d])
            hand(m, h, 4 + 3 * j + 2, col, row)

    p1_far(0)
    p1_early(0)
    p1_late(0)
    p1_far(1)
    p1_end(0)
    p2_first(0)
    p1_early(1)
    p2_late(0)
    p1_late(1)
    p2_end(0)
    p1_end(1)
    p2_first(1)
    gram_sum(0)
    p2_late(1)
    update(0)
    g_start(0)
    p2_end(1)
    g_first(0)
    gram_sum(1)
    g_far(0)
    g_pass(0, 0)
    update(1)
    g_start(1)
    g_last(0, 0)
    g_pass(0, 1)
    g_pass(0, 2)
    g_first(1)
    g_pass(0, 3)
    g_far(1)
    g_last(0, 1)
    g_last(0, 2)
    g_last(0, 3)
    for j in range(4):
        g_pass(1, j)
    for j in range(4):
        g_last(1, j)
    for m in range(2):
        theirs = outs[m].at[:, :, other]
        landed(theirs, as_rs.at[m])
    for copy in sends:
        copy.wait_send()


def call(nz, width, *args):
    f32, bf16 = jnp.float32, jnp.bfloat16
    dma = pltpu.SemaphoreType.DMA
    vmem = pl.BlockSpec(memory_space=pltpu.VMEM)
    hbm = pl.BlockSpec(memory_space=pl.ANY)
    out = jax.ShapeDtypeStruct((NX, NY, NC, BLK, width), bf16)
    new = jax.ShapeDtypeStruct((BLK, width), f32)
    group = BLK // nz
    return pl.pallas_call(
        functools.partial(kernel, nz, width),
        out_shape=(new, new, out, out),
        in_specs=[hbm] * 6,
        out_specs=(vmem,) * 4,
        scratch_shapes=[
            pltpu.VMEM((4, 4, 4, HALF, width), bf16),
            pltpu.VMEM((4, 4, 4, HALF, width), bf16),
            pltpu.VMEM((4, 2, 4, QUART, width), WIRE),
            pltpu.VMEM((4, 2, 4, QUART, width), WIRE),
            pltpu.VMEM((4, 2, 2, 4, QUART, width), WIRE),
            pltpu.VMEM((4, 2, 2, 4, QUART, width), WIRE),
            pltpu.VMEM((4, 4, HALF, width), f32),
            pltpu.VMEM((4, 2, QUART, width), f32),
            pltpu.VMEM((4, 2, 2, QUART, width), f32),
            pltpu.VMEM((2, BLK, width), f32),
            pltpu.VMEM((2, BLK, width), f32),
            pltpu.VMEM((2, BLK, width), f32),
            pltpu.VMEM((2, nz, group, BLK), f32),
            pltpu.VMEM((2, nz - 1, group, BLK), f32),
            pltpu.VMEM((2, nz, group, BLK), f32),
            dma((2, 2)), dma((4, 4)), dma((4, 4)), dma((4, 4)),
            dma((4, 2, 3)), dma((4, 2, 3)), dma((4, 2, 3)), dma((4, 2, 3)),
            dma((2, nz - 1)), dma((2,)), dma((2, nz - 1)), dma((2,)),
            dma((4, 4)), dma((4, 4)), dma((4, 4, 4)), dma((4, 4, 4)), dma((4, 16)), dma((2,)),
        ],
        compiler_params=pltpu.CompilerParams(
            collective_id=0, has_side_effects=True, vmem_limit_bytes=60 * 1024 * 1024
        ),
    )(*args)


def body(grad_down, grad_out, momentum_down, momentum_out, master_down, master_out):
    nz = lax.axis_size("mp")
    width = grad_down.shape[-1]
    shape = (NX, NY, NC, BLK, width)
    new_down, new_out, out_down, out_out = call(
        nz, width, grad_down.reshape(shape), grad_out.reshape(shape),
        momentum_down, momentum_out, master_down, master_out,
    )
    rows = NX * NY * NC * BLK
    return (new_down, new_out, out_down.reshape(rows, width), out_out.reshape(rows, width))


def solution(mesh):
    placed = (
        P("dp", None, "mp"),
        P("dp", None, "mp"),
        P("dp", "mp"),
        P("dp", "mp"),
        P("dp", "mp"),
        P("dp", "mp"),
    )
    return jax.shard_map(
        body,
        mesh=mesh,
        in_specs=placed,
        out_specs=(P("dp", "mp"), P("dp", "mp"), P(None, "mp"), P(None, "mp")),
        check_vma=False,
    )
```

```python
import functools
import math

import jax
import jax.numpy as jnp
from jax import lax
from jax.experimental import pallas as pl
from jax.experimental.pallas import tpu as pltpu
from jax.sharding import PartitionSpec as P

D = 5120
BLK = 128
ITERS = 3
NX, NY, NC = 4, 4, 2
HALF = 64
TOP = 6.0
QUART = 32
MESH = pl.DeviceIdType.MESH

momentum_coef = 0.95
learn_rate = 0.5
decay_rate = 0.1
coef_a = 3.4445
coef_b = -4.775
coef_c = 2.0315
norm_eps = 1e-07

WIRE = jnp.bfloat16
POWER = 12
LOW, HIGH = 2.0**-10.4, 2.0**10.4


def encode(x, bound):
    v = jnp.abs(x) * ((HIGH - LOW) / bound) + LOW
    v = v * v * v
    v = v * v
    v = v * v
    return jnp.where(x < 0, -v, v).astype(WIRE)


def decode(y, bound):
    w = y.astype(jnp.float32)
    v = jnp.exp2(jnp.log(jnp.abs(w)) * (1.0 / (POWER * math.log(2.0))))
    v = (v - LOW) * (bound / (HIGH - LOW))
    return jnp.where(w < 0, -v, v)


STEPS = (
    ("far", 0),
    ("early", 0),
    ("late", 0),
    ("far", 1),
    ("end", 0),
    ("first2", 0),
    ("early", 1),
    ("late2", 0),
    ("late", 1),
    ("end2", 0),
    ("gram_send", 0),
    ("end", 1),
    ("first2", 1),
    ("gram_sum", 0),
    ("late2", 1),
    ("update", 0),
    ("g_start", 0),
    ("end2", 1),
    ("gram_send", 1),
    ("g_first", 0),
    ("gram_sum", 1),
    ("g_far", 0),
    ("g_pass", 0, 0),
    ("update", 1),
    ("g_start", 1),
    ("g_last", 0, 0),
    ("g_pass", 0, 1),
    ("g_pass", 0, 2),
    ("g_first", 1),
    ("g_pass", 0, 3),
    ("g_far", 1),
    ("g_last", 0, 1),
    ("g_last", 0, 2),
    ("g_last", 0, 3),
    ("g_pass", 1, 0),
    ("g_pass", 1, 1),
    ("g_pass", 1, 2),
    ("g_pass", 1, 3),
    ("g_last", 1, 0),
    ("g_last", 1, 1),
    ("g_last", 1, 2),
    ("g_last", 1, 3),
    ("g_end", 0),
    ("g_end", 1),
)


def dot(a, b):
    return jnp.dot(a, b, precision=lax.Precision.HIGHEST, preferred_element_type=jnp.float32)


def kernel(
    nz, width,
    grad_down, grad_out, mom_down, mom_out, mas_down, mas_out,
    new_down, new_out, out_down, out_out,
    own, sib, s2, r2, s1, r1, acc, rr2, rr1, mom, mas, look, gpart, gslot, gfull,
    small_sem, own_sem, sib_ss, sib_rs,
    p1_ss, p1_rs, p2_ss, p2_rs,
    ga_ss, ga_rs, gb_ss, gb_rs,
    aa_ss, aa_rs, ab_ss, ab_rs, as_ss, as_rs,
):
    grads, moms, mass = (grad_down, grad_out), (mom_down, mom_out), (mas_down, mas_out)
    news, outs = (new_down, new_out), (out_down, out_out)
    dp, z = lax.axis_index("dp"), lax.axis_index("mp")
    c = lax.rem(dp, 2)
    chip = lax.div(dp, 2)
    y = lax.rem(chip, NY)
    x = lax.div(chip, NY)
    other = 1 - c

    def wrap(v):
        return lax.rem(v + 4, 4)

    def device(px, py, pc=c, pz=z):
        return ((px * NY + py) * NC + pc, pz)

    sibling = device(x, y, other)
    pos = ((x, y), (y, x))

    def along(h, axis, step):
        use_x = (axis == 0) == (h == 0)
        return device(wrap(x + step), y) if use_x else device(x, wrap(y + step))

    def chip_at(h, a, b):
        return (a, b) if h == 0 else (b, a)

    def remote(src, dst, ss, rs, dev):
        return pltpu.make_async_remote_copy(
            src_ref=src, dst_ref=dst, send_sem=ss, recv_sem=rs, device_id=dev, device_id_type=MESH
        )

    sends = []

    def send(src, dst, ss, rs, dev):
        copy = remote(src, dst, ss, rs, dev)
        copy.start()
        sends.append(copy)

    def landed(dst, rs):
        pltpu.make_async_copy(dst, dst, rs).wait()

    order = (2, 1, 3, 0)

    def source(m, h, da, core):
        a = wrap(pos[h][0] + da)
        if h == 0:
            return grads[m].at[a, :, core, 0:HALF, :]
        return grads[m].at[:, a, core, HALF:BLK, :]

    own_copies = {}
    for m in range(2):
        for da in order:
            for h in range(2):
                mh = 2 * m + h
                copy = pltpu.make_async_copy(source(m, h, da, c), own.at[mh, da], own_sem.at[mh, da])
                copy.start()
                own_copies[mh, da] = copy
    small = []
    for m in range(2):
        for k, (src, dst) in enumerate(((moms[m], mom.at[m]), (mass[m], mas.at[m]))):
            copy = pltpu.make_async_copy(src, dst, small_sem.at[m, k])
            copy.start()
            small.append(copy)

    barrier = pltpu.get_barrier_semaphore()
    peers = [sibling]
    for h in range(2):
        peers += [along(h, 0, 1), along(h, 0, -1)]
    peers += [device(x, y, c, lax.rem(z + k, nz)) for k in range(1, nz)]
    for peer in peers:
        pl.semaphore_signal(barrier, inc=1, device_id=peer, device_id_type=MESH)
    pl.semaphore_wait(barrier, len(peers))

    for m in range(2):
        for da in order:
            for h in range(2):
                mh = 2 * m + h
                send(source(m, h, da, other), sib.at[mh, da], sib_ss.at[mh, da], sib_rs.at[mh, da], sibling)

    def have(m, da):
        for h in range(2):
            own_copies[2 * m + h, da].wait()
            landed(sib.at[2 * m + h, da], sib_rs.at[2 * m + h, da])

    def pair(mh, da, b, lo):
        rows = pl.ds(lo, QUART)
        return own[mh, da, b, rows, :].astype(jnp.float32) + sib[mh, da, b, rows, :].astype(jnp.float32)

    def p1_far(m):
        have(m, 2)
        for h in range(2):
            mh = 2 * m + h
            for d in range(2):
                @pl.loop(0, 4)
                def _(b):
                    s2[mh, d, b] = encode(pair(mh, 2, b, QUART * d), 2 * TOP)
                send(s2.at[mh, d], r2.at[mh, d], p1_ss.at[mh, d, 0], p1_rs.at[mh, d, 0], along(h, 0, 1 - 2 * d))

    def p1_early(m):
        have(m, 1)
        have(m, 3)
        for h in range(2):
            mh = 2 * m + h
            for d in range(2):
                @pl.loop(0, 4)
                def _(b):
                    s1[mh, d, 0, b] = encode(pair(mh, 1 + 2 * d, b, QUART * (1 - d)), 2 * TOP)
                send(s1.at[mh, d, 0], r1.at[mh, d, 0], p1_ss.at[mh, d, 1], p1_rs.at[mh, d, 1], along(h, 0, 1 - 2 * d))

    def p1_late(m):
        for h in range(2):
            mh = 2 * m + h
            for d in range(2):
                landed(r2.at[mh, d], p1_rs.at[mh, d, 0])

                @pl.loop(0, 4)
                def _(b):
                    s1[mh, d, 1, b] = encode(
                        pair(mh, 1 + 2 * d, b, QUART * d) + decode(r2[mh, d, b], 2 * TOP), 4 * TOP
                    )
                send(s1.at[mh, d, 1], r1.at[mh, d, 1], p1_ss.at[mh, d, 2], p1_rs.at[mh, d, 2], along(h, 0, 1 - 2 * d))

    def p1_end(m):
        have(m, 0)
        for h in range(2):
            mh = 2 * m + h
            for d in range(2):
                for e in range(2):
                    landed(r1.at[mh, d, e], p1_rs.at[mh, d, 1 + e])

            @pl.loop(0, 4)
            def _(b):
                for q in range(2):
                    acc[mh, b, pl.ds(QUART * q, QUART), :] = (
                        pair(mh, 0, b, QUART * q)
                        + decode(r1[mh, q, 1, b], 4 * TOP) + decode(r1[mh, 1 - q, 0, b], 2 * TOP)
                    )

    def p2_first(m):
        for h in range(2):
            mh = 2 * m + h
            at = pos[h][1]
            for d in range(2):
                to = along(h, 1, 1 - 2 * d)
                far = acc.at[mh, wrap(at + 2), pl.ds(QUART * d, QUART), :]
                send(far, rr2.at[mh, d], p2_ss.at[mh, d, 0], p2_rs.at[mh, d, 0], to)
            for d in range(2):
                to = along(h, 1, 1 - 2 * d)
                near = acc.at[mh, wrap(at + 1 - 2 * d), pl.ds(QUART * (1 - d), QUART), :]
                send(near, rr1.at[mh, d, 0], p2_ss.at[mh, d, 1], p2_rs.at[mh, d, 1], to)

    def p2_late(m):
        for h in range(2):
            mh = 2 * m + h
            for d in range(2):
                landed(rr2.at[mh, d], p2_rs.at[mh, d, 0])
                near = acc.at[mh, wrap(pos[h][1] + 1 - 2 * d), pl.ds(QUART * d, QUART), :]
                near[...] = near[...] + rr2[mh, d]
                send(near, rr1.at[mh, d, 1], p2_ss.at[mh, d, 2], p2_rs.at[mh, d, 2], along(h, 1, 1 - 2 * d))

    def p2_end(m):
        if m == 0:
            for copy in small:
                copy.wait()
        for h in range(2):
            mh = 2 * m + h
            for d in range(2):
                for e in range(2):
                    landed(rr1.at[mh, d, e], p2_rs.at[mh, d, 1 + e])
            for q in range(2):
                rows = pl.ds(HALF * h + QUART * q, QUART)
                total = acc[mh, pos[h][1], pl.ds(QUART * q, QUART), :] + rr1[mh, q, 1] + rr1[mh, 1 - q, 0]
                new = momentum_coef * mom[m, rows, :] + total
                news[m][rows, :] = new
                look[m, rows, :] = total + momentum_coef * new

    def gram_send(m):
        u = look[m]
        gram = lax.dot_general(
            u, u, (((1,), (1,)), ((), ())),
            precision=lax.Precision.HIGHEST, preferred_element_type=jnp.float32,
        )
        gpart[m] = gram.reshape(nz, BLK // nz, BLK)
        for k in range(1, nz):
            to = lax.rem(z + k, nz)
            send(gpart.at[m, to], gslot.at[m, k - 1], ga_ss.at[m, k - 1], ga_rs.at[m], device(x, y, c, to))

    def gram_sum(m):
        landed(gslot.at[m], ga_rs.at[m])
        total = gpart[m, z]
        for k in range(nz - 1):
            total = total + gslot[m, k]
        gfull[m, z] = total
        for k in range(1, nz):
            to = lax.rem(z + k, nz)
            send(gfull.at[m, z], gfull.at[m, z], gb_ss.at[m, k - 1], gb_rs.at[m], device(x, y, c, to))

    def update(m):
        landed(gslot.at[m], gb_rs.at[m])
        gram = gfull[m].reshape(BLK, BLK)
        eye = lax.broadcasted_iota(jnp.int32, (BLK, BLK), 0) == lax.broadcasted_iota(jnp.int32, (BLK, BLK), 1)
        diag = jnp.where(eye, gram, 0.0)
        square = jnp.sum(jnp.sum(diag, axis=1, keepdims=True), axis=0, keepdims=True)
        inv = 1.0 / (jnp.sqrt(square) + norm_eps)
        gram = gram * inv * inv
        ident = jnp.where(eye, coef_a, 0.0)
        whole = None
        for step in range(ITERS):
            factor = ident + coef_b * gram + coef_c * dot(gram, gram)
            whole = factor if whole is None else dot(factor, whole)
            if step < ITERS - 1:
                gram = dot(dot(factor, gram), factor)
        ortho = dot(whole * inv, look[m])
        scale = learn_rate * 0.2 * math.sqrt(D)
        weights = (1.0 - learn_rate * decay_rate) * mas[m] - scale * ortho
        outs[m][x, y, c] = weights.astype(jnp.bfloat16)

    def block(m, h, a, b, lo=0, n=HALF):
        px, py = chip_at(h, a, b)
        return outs[m].at[px, py, c, pl.ds(HALF * h + lo, n), :]

    def hand(m, h, k, a, b):
        ref = block(m, h, a, b)
        send(ref, ref, as_ss.at[2 * m + h, k], as_rs.at[m], sibling)

    def fan(m, h, j, a):
        mh, ref = 2 * m + h, block(m, h, a, pos[h][1])
        for d in range(2):
            send(ref, ref, ab_ss.at[mh, j, d], ab_rs.at[mh, j, d], along(h, 1, 1 - 2 * d))

    def cols(h):
        a = pos[h][0]
        return (a, wrap(a - 1), wrap(a + 1), wrap(a + 2))

    def g_start(m):
        for h in range(2):
            mh, (a, b) = 2 * m + h, pos[h]
            ref = block(m, h, a, b)
            for d in range(2):
                send(ref, ref, aa_ss.at[mh, d], aa_rs.at[mh, d], along(h, 0, 1 - 2 * d))
        for h in range(2):
            fan(m, h, 0, pos[h][0])
            hand(m, h, 0, *pos[h])

    def g_first(m):
        for h in range(2):
            mh, (a, b) = 2 * m + h, pos[h]
            for d in range(2):
                col = cols(h)[1 + d]
                ref = block(m, h, col, b)
                landed(ref, aa_rs.at[mh, d])
                part = block(m, h, col, b, QUART * d, QUART)
                send(part, part, aa_ss.at[mh, 2 + d], aa_rs.at[mh, 2 + d], along(h, 0, 1 - 2 * d))
                fan(m, h, 1 + d, col)
                hand(m, h, 1 + d, col, b)

    def g_far(m):
        for h in range(2):
            mh, (a, b) = 2 * m + h, pos[h]
            col = cols(h)[3]
            for d in range(2):
                landed(block(m, h, col, b, QUART * d, QUART), aa_rs.at[mh, 2 + d])
            fan(m, h, 3, col)
            hand(m, h, 3, col, b)

    def g_pass(m, j):
        for h in range(2):
            mh, b = 2 * m + h, pos[h][1]
            col = cols(h)[j]
            for d in range(2):
                row = wrap(b - 1 + 2 * d)
                landed(block(m, h, col, row), ab_rs.at[mh, j, d])
                part = block(m, h, col, row, QUART * d, QUART)
                send(part, part, ab_ss.at[mh, j, 2 + d], ab_rs.at[mh, j, 2 + d], along(h, 1, 1 - 2 * d))
                hand(m, h, 4 + 3 * j + d, col, row)

    def g_last(m, j):
        for h in range(2):
            mh, b = 2 * m + h, pos[h][1]
            col, row = cols(h)[j], wrap(b + 2)
            for d in range(2):
                landed(block(m, h, col, row, QUART * d, QUART), ab_rs.at[mh, j, 2 + d])
            hand(m, h, 4 + 3 * j + 2, col, row)

    def g_end(m):
        landed(outs[m].at[:, :, other], as_rs.at[m])

    steps = dict(
        far=p1_far, early=p1_early, late=p1_late, end=p1_end, first2=p2_first, late2=p2_late, end2=p2_end,
        gram_send=gram_send, gram_sum=gram_sum, update=update, g_start=g_start, g_first=g_first, g_far=g_far,
        g_pass=g_pass, g_last=g_last, g_end=g_end,
    )
    for name, *at in STEPS:
        steps[name](*at)
    for copy in sends:
        copy.wait_send()


def call(nz, width, *args):
    f32, bf16 = jnp.float32, jnp.bfloat16
    dma = pltpu.SemaphoreType.DMA
    vmem = pl.BlockSpec(memory_space=pltpu.VMEM)
    hbm = pl.BlockSpec(memory_space=pl.ANY)
    out = pltpu.VMEM((NX, NY, NC, BLK, width), bf16)
    new = pltpu.VMEM((BLK, width), f32)
    group = BLK // nz
    return pl.pallas_call(
        functools.partial(kernel, nz, width),
        out_shape=(new, new, out, out),
        in_specs=[hbm] * 6,
        out_specs=(vmem,) * 4,
        scratch_shapes=[
            pltpu.VMEM((4, 4, 4, HALF, width), bf16),
            pltpu.VMEM((4, 4, 4, HALF, width), bf16),
            pltpu.VMEM((4, 2, 4, QUART, width), WIRE),
            pltpu.VMEM((4, 2, 4, QUART, width), WIRE),
            pltpu.VMEM((4, 2, 2, 4, QUART, width), WIRE),
            pltpu.VMEM((4, 2, 2, 4, QUART, width), WIRE),
            pltpu.VMEM((4, 4, HALF, width), f32),
            pltpu.VMEM((4, 2, QUART, width), f32),
            pltpu.VMEM((4, 2, 2, QUART, width), f32),
            pltpu.VMEM((2, BLK, width), f32),
            pltpu.VMEM((2, BLK, width), f32),
            pltpu.VMEM((2, BLK, width), f32),
            pltpu.VMEM((2, nz, group, BLK), f32),
            pltpu.VMEM((2, nz - 1, group, BLK), f32),
            pltpu.VMEM((2, nz, group, BLK), f32),
            dma((2, 2)), dma((4, 4)), dma((4, 4)), dma((4, 4)),
            dma((4, 2, 3)), dma((4, 2, 3)), dma((4, 2, 3)), dma((4, 2, 3)),
            dma((2, nz - 1)), dma((2,)), dma((2, nz - 1)), dma((2,)),
            dma((4, 4)), dma((4, 4)), dma((4, 4, 4)), dma((4, 4, 4)), dma((4, 16)), dma((2,)),
        ],
        compiler_params=pltpu.CompilerParams(
            collective_id=0, has_side_effects=True, vmem_limit_bytes=44 * 1024 * 1024
        ),
    )(*args)


def store_kernel(*refs):
    sem = refs[-1]
    copies = [pltpu.make_async_copy(refs[k], refs[4 + k], sem.at[k]) for k in range(4)]
    for copy in copies:
        copy.start()
    for copy in copies:
        copy.wait()


def store(*held):
    return pl.pallas_call(
        store_kernel,
        out_shape=tuple(jax.ShapeDtypeStruct(h.shape, h.dtype) for h in held),
        in_specs=[pl.BlockSpec(memory_space=pltpu.VMEM)] * 4,
        out_specs=(pl.BlockSpec(memory_space=pl.ANY),) * 4,
        scratch_shapes=[pltpu.SemaphoreType.DMA((4,))],
    )(*held)


def body(grad_down, grad_out, momentum_down, momentum_out, master_down, master_out):
    nz = lax.axis_size("mp")
    width = grad_down.shape[-1]
    shape = (NX, NY, NC, BLK, width)
    new_down, new_out, out_down, out_out = store(*call(
        nz, width, grad_down.reshape(shape), grad_out.reshape(shape),
        momentum_down, momentum_out, master_down, master_out,
    ))
    rows = NX * NY * NC * BLK
    return (new_down, new_out, out_down.reshape(rows, width), out_out.reshape(rows, width))


def solution(mesh):
    placed = (
        P("dp", None, "mp"),
        P("dp", None, "mp"),
        P("dp", "mp"),
        P("dp", "mp"),
        P("dp", "mp"),
        P("dp", "mp"),
    )
    return jax.shard_map(
        body,
        mesh=mesh,
        in_specs=placed,
        out_specs=(P("dp", "mp"), P("dp", "mp"), P(None, "mp"), P(None, "mp")),
        check_vma=False,
    )
```

```python
import functools
import math

import jax
import jax.numpy as jnp
from jax import lax
from jax.experimental import pallas as pl
from jax.experimental.pallas import tpu as pltpu
from jax.sharding import PartitionSpec as P

D = 5120
BLK = 128
ITERS = 3
NX, NY, NC = 4, 4, 2
HALF = 64
TOP = 6.0
QUART = 32
MESH = pl.DeviceIdType.MESH

momentum_coef = 0.95
learn_rate = 0.5
decay_rate = 0.1
coef_a = 3.4445
coef_b = -4.775
coef_c = 2.0315
norm_eps = 1e-07

WIRE = jnp.bfloat16
POWER = 12
LOW, HIGH = 2.0**-10.4, 2.0**10.4


def encode(x, bound):
    v = jnp.abs(x) * ((HIGH - LOW) / bound) + LOW
    v = v * v * v
    v = v * v
    v = v * v
    return jnp.where(x < 0, -v, v).astype(WIRE)


def decode(y, bound):
    w = y.astype(jnp.float32)
    v = jnp.exp2(jnp.log(jnp.abs(w)) * (1.0 / (POWER * math.log(2.0))))
    v = (v - LOW) * (bound / (HIGH - LOW))
    return jnp.where(w < 0, -v, v)


STEPS = (
    ("far", 0),
    ("early", 0),
    ("late", 0),
    ("far", 1),
    ("end", 0),
    ("first2", 0),
    ("early", 1),
    ("late2", 0),
    ("late", 1),
    ("end2", 0),
    ("gram_send", 0),
    ("end", 1),
    ("first2", 1),
    ("gram_sum", 0),
    ("late2", 1),
    ("update", 0),
    ("g_start", 0),
    ("end2", 1),
    ("gram_send", 1),
    ("g_first", 0),
    ("gram_sum", 1),
    ("g_far", 0),
    ("g_pass", 0, 0),
    ("update", 1),
    ("g_start", 1),
    ("g_last", 0, 0),
    ("g_pass", 0, 1),
    ("g_pass", 0, 2),
    ("g_first", 1),
    ("g_pass", 0, 3),
    ("g_far", 1),
    ("g_last", 0, 1),
    ("g_last", 0, 2),
    ("g_last", 0, 3),
    ("g_pass", 1, 0),
    ("g_pass", 1, 1),
    ("g_pass", 1, 2),
    ("g_pass", 1, 3),
    ("g_last", 1, 0),
    ("g_last", 1, 1),
    ("g_last", 1, 2),
    ("g_last", 1, 3),
    ("g_end", 0),
    ("g_end", 1),
)


def dot(a, b):
    return jnp.dot(a, b, precision=lax.Precision.HIGHEST, preferred_element_type=jnp.float32)


def kernel(
    nz, width,
    grad_down, grad_out, mom_down, mom_out, mas_down, mas_out,
    new_down, new_out, out_down, out_out,
    own, sib, s2, r2, s1, r1, acc, rr2, rr1, mom, mas, look, gpart, gslot, gfull,
    small_sem, own_sem, sib_ss, sib_rs,
    p1_ss, p1_rs, p2_ss, p2_rs,
    ga_ss, ga_rs, gb_ss, gb_rs,
    aa_ss, aa_rs, ab_ss, ab_rs, as_ss, as_rs,
):
    grads, moms, mass = (grad_down, grad_out), (mom_down, mom_out), (mas_down, mas_out)
    news, outs = (new_down, new_out), (out_down, out_out)
    dp, z = lax.axis_index("dp"), lax.axis_index("mp")
    c = lax.rem(dp, 2)
    chip = lax.div(dp, 2)
    y = lax.rem(chip, NY)
    x = lax.div(chip, NY)
    other = 1 - c

    def wrap(v):
        return lax.rem(v + 4, 4)

    def device(px, py, pc=c, pz=z):
        return ((px * NY + py) * NC + pc, pz)

    sibling = device(x, y, other)
    pos = ((x, y), (y, x))

    def along(h, axis, step):
        use_x = (axis == 0) == (h == 0)
        return device(wrap(x + step), y) if use_x else device(x, wrap(y + step))

    def chip_at(h, a, b):
        return (a, b) if h == 0 else (b, a)

    def remote(src, dst, ss, rs, dev):
        return pltpu.make_async_remote_copy(
            src_ref=src, dst_ref=dst, send_sem=ss, recv_sem=rs, device_id=dev, device_id_type=MESH
        )

    sends = []

    def send(src, dst, ss, rs, dev):
        copy = remote(src, dst, ss, rs, dev)
        copy.start()
        sends.append(copy)

    def landed(dst, rs):
        pltpu.make_async_copy(dst, dst, rs).wait()

    order = (2, 1, 3, 0)

    def source(m, h, da, core):
        a = wrap(pos[h][0] + da)
        if h == 0:
            return grads[m].at[a, :, core, 0:HALF, :]
        return grads[m].at[:, a, core, HALF:BLK, :]

    own_copies = {}
    for m in range(2):
        for da in order:
            for h in range(2):
                mh = 2 * m + h
                copy = pltpu.make_async_copy(source(m, h, da, c), own.at[mh, da], own_sem.at[mh, da])
                copy.start()
                own_copies[mh, da] = copy
    small = []
    for m in range(2):
        for k, (src, dst) in enumerate(((moms[m], mom.at[m]), (mass[m], mas.at[m]))):
            copy = pltpu.make_async_copy(src, dst, small_sem.at[m, k])
            copy.start()
            small.append(copy)

    barrier = pltpu.get_barrier_semaphore()
    peers = [sibling]
    for h in range(2):
        peers += [along(h, 0, 1), along(h, 0, -1)]
    peers += [device(x, y, c, lax.rem(z + k, nz)) for k in range(1, nz)]
    for peer in peers:
        pl.semaphore_signal(barrier, inc=1, device_id=peer, device_id_type=MESH)
    pl.semaphore_wait(barrier, len(peers))

    for m in range(2):
        for da in order:
            for h in range(2):
                mh = 2 * m + h
                send(source(m, h, da, other), sib.at[mh, da], sib_ss.at[mh, da], sib_rs.at[mh, da], sibling)

    def have(m, da):
        for h in range(2):
            own_copies[2 * m + h, da].wait()
            landed(sib.at[2 * m + h, da], sib_rs.at[2 * m + h, da])

    def pair(mh, da, b, lo):
        rows = pl.ds(lo, QUART)
        return own[mh, da, b, rows, :].astype(jnp.float32) + sib[mh, da, b, rows, :].astype(jnp.float32)

    def p1_far(m):
        have(m, 2)
        for h in range(2):
            mh = 2 * m + h
            for d in range(2):
                @pl.loop(0, 4)
                def _(b):
                    s2[mh, d, b] = encode(pair(mh, 2, b, QUART * d), 2 * TOP)
                send(s2.at[mh, d], r2.at[mh, d], p1_ss.at[mh, d, 0], p1_rs.at[mh, d, 0], along(h, 0, 1 - 2 * d))

    def p1_early(m):
        have(m, 1)
        have(m, 3)
        for h in range(2):
            mh = 2 * m + h
            for d in range(2):
                @pl.loop(0, 4)
                def _(b):
                    s1[mh, d, 0, b] = encode(pair(mh, 1 + 2 * d, b, QUART * (1 - d)), 2 * TOP)
                send(s1.at[mh, d, 0], r1.at[mh, d, 0], p1_ss.at[mh, d, 1], p1_rs.at[mh, d, 1], along(h, 0, 1 - 2 * d))

    def p1_late(m):
        for h in range(2):
            mh = 2 * m + h
            for d in range(2):
                landed(r2.at[mh, d], p1_rs.at[mh, d, 0])

                @pl.loop(0, 4)
                def _(b):
                    s1[mh, d, 1, b] = encode(
                        pair(mh, 1 + 2 * d, b, QUART * d) + decode(r2[mh, d, b], 2 * TOP), 4 * TOP
                    )
                send(s1.at[mh, d, 1], r1.at[mh, d, 1], p1_ss.at[mh, d, 2], p1_rs.at[mh, d, 2], along(h, 0, 1 - 2 * d))

    def p1_end(m):
        have(m, 0)
        for h in range(2):
            mh = 2 * m + h
            for d in range(2):
                for e in range(2):
                    landed(r1.at[mh, d, e], p1_rs.at[mh, d, 1 + e])

            @pl.loop(0, 4)
            def _(b):
                for q in range(2):
                    acc[mh, b, pl.ds(QUART * q, QUART), :] = (
                        pair(mh, 0, b, QUART * q)
                        + decode(r1[mh, q, 1, b], 4 * TOP) + decode(r1[mh, 1 - q, 0, b], 2 * TOP)
                    )

    def p2_first(m):
        for h in range(2):
            mh = 2 * m + h
            at = pos[h][1]
            for d in range(2):
                to = along(h, 1, 1 - 2 * d)
                far = acc.at[mh, wrap(at + 2), pl.ds(QUART * d, QUART), :]
                send(far, rr2.at[mh, d], p2_ss.at[mh, d, 0], p2_rs.at[mh, d, 0], to)
            for d in range(2):
                to = along(h, 1, 1 - 2 * d)
                near = acc.at[mh, wrap(at + 1 - 2 * d), pl.ds(QUART * (1 - d), QUART), :]
                send(near, rr1.at[mh, d, 0], p2_ss.at[mh, d, 1], p2_rs.at[mh, d, 1], to)

    def p2_late(m):
        for h in range(2):
            mh = 2 * m + h
            for d in range(2):
                landed(rr2.at[mh, d], p2_rs.at[mh, d, 0])
                near = acc.at[mh, wrap(pos[h][1] + 1 - 2 * d), pl.ds(QUART * d, QUART), :]
                near[...] = near[...] + rr2[mh, d]
                send(near, rr1.at[mh, d, 1], p2_ss.at[mh, d, 2], p2_rs.at[mh, d, 2], along(h, 1, 1 - 2 * d))

    def p2_end(m):
        if m == 0:
            for copy in small:
                copy.wait()
        for h in range(2):
            mh = 2 * m + h
            for d in range(2):
                for e in range(2):
                    landed(rr1.at[mh, d, e], p2_rs.at[mh, d, 1 + e])
            for q in range(2):
                rows = pl.ds(HALF * h + QUART * q, QUART)
                total = acc[mh, pos[h][1], pl.ds(QUART * q, QUART), :] + rr1[mh, q, 1] + rr1[mh, 1 - q, 0]
                new = momentum_coef * mom[m, rows, :] + total
                news[m][rows, :] = new
                look[m, rows, :] = total + momentum_coef * new

    def gram_send(m):
        u = look[m]
        gram = lax.dot_general(
            u, u, (((1,), (1,)), ((), ())),
            precision=lax.Precision.HIGHEST, preferred_element_type=jnp.float32,
        )
        gpart[m] = gram.reshape(nz, BLK // nz, BLK)
        for k in range(1, nz):
            to = lax.rem(z + k, nz)
            send(gpart.at[m, to], gslot.at[m, k - 1], ga_ss.at[m, k - 1], ga_rs.at[m], device(x, y, c, to))

    def gram_sum(m):
        landed(gslot.at[m], ga_rs.at[m])
        total = gpart[m, z]
        for k in range(nz - 1):
            total = total + gslot[m, k]
        gfull[m, z] = total
        for k in range(1, nz):
            to = lax.rem(z + k, nz)
            send(gfull.at[m, z], gfull.at[m, z], gb_ss.at[m, k - 1], gb_rs.at[m], device(x, y, c, to))

    def update(m):
        landed(gslot.at[m], gb_rs.at[m])
        gram = gfull[m].reshape(BLK, BLK)
        eye = lax.broadcasted_iota(jnp.int32, (BLK, BLK), 0) == lax.broadcasted_iota(jnp.int32, (BLK, BLK), 1)
        diag = jnp.where(eye, gram, 0.0)
        square = jnp.sum(jnp.sum(diag, axis=1, keepdims=True), axis=0, keepdims=True)
        inv = 1.0 / (jnp.sqrt(square) + norm_eps)
        gram = gram * inv * inv
        ident = jnp.where(eye, coef_a, 0.0)
        whole = None
        for step in range(ITERS):
            factor = ident + coef_b * gram + coef_c * dot(gram, gram)
            whole = factor if whole is None else dot(factor, whole)
            if step < ITERS - 1:
                gram = dot(dot(factor, gram), factor)
        ortho = dot(whole * inv, look[m])
        scale = learn_rate * 0.2 * math.sqrt(D)
        weights = (1.0 - learn_rate * decay_rate) * mas[m] - scale * ortho
        outs[m][x, y, c] = weights.astype(jnp.bfloat16)

    def block(m, h, a, b, lo=0, n=HALF):
        px, py = chip_at(h, a, b)
        return outs[m].at[px, py, c, pl.ds(HALF * h + lo, n), :]

    def hand(m, h, k, a, b):
        ref = block(m, h, a, b)
        send(ref, ref, as_ss.at[2 * m + h, k], as_rs.at[m], sibling)

    def fan(m, h, j, a):
        mh, ref = 2 * m + h, block(m, h, a, pos[h][1])
        for d in range(2):
            send(ref, ref, ab_ss.at[mh, j, d], ab_rs.at[mh, j, d], along(h, 1, 1 - 2 * d))

    def cols(h):
        a = pos[h][0]
        return (a, wrap(a - 1), wrap(a + 1), wrap(a + 2))

    def g_start(m):
        for h in range(2):
            mh, (a, b) = 2 * m + h, pos[h]
            ref = block(m, h, a, b)
            for d in range(2):
                send(ref, ref, aa_ss.at[mh, d], aa_rs.at[mh, d], along(h, 0, 1 - 2 * d))
        for h in range(2):
            fan(m, h, 0, pos[h][0])
            hand(m, h, 0, *pos[h])

    def g_first(m):
        for h in range(2):
            mh, (a, b) = 2 * m + h, pos[h]
            for d in range(2):
                col = cols(h)[1 + d]
                ref = block(m, h, col, b)
                landed(ref, aa_rs.at[mh, d])
                part = block(m, h, col, b, QUART * d, QUART)
                send(part, part, aa_ss.at[mh, 2 + d], aa_rs.at[mh, 2 + d], along(h, 0, 1 - 2 * d))
                fan(m, h, 1 + d, col)
                hand(m, h, 1 + d, col, b)

    def g_far(m):
        for h in range(2):
            mh, (a, b) = 2 * m + h, pos[h]
            col = cols(h)[3]
            for d in range(2):
                landed(block(m, h, col, b, QUART * d, QUART), aa_rs.at[mh, 2 + d])
            fan(m, h, 3, col)
            hand(m, h, 3, col, b)

    def g_pass(m, j):
        for h in range(2):
            mh, b = 2 * m + h, pos[h][1]
            col = cols(h)[j]
            for d in range(2):
                row = wrap(b - 1 + 2 * d)
                landed(block(m, h, col, row), ab_rs.at[mh, j, d])
                part = block(m, h, col, row, QUART * d, QUART)
                send(part, part, ab_ss.at[mh, j, 2 + d], ab_rs.at[mh, j, 2 + d], along(h, 1, 1 - 2 * d))
                hand(m, h, 4 + 3 * j + d, col, row)

    def g_last(m, j):
        for h in range(2):
            mh, b = 2 * m + h, pos[h][1]
            col, row = cols(h)[j], wrap(b + 2)
            for d in range(2):
                landed(block(m, h, col, row, QUART * d, QUART), ab_rs.at[mh, j, 2 + d])
            hand(m, h, 4 + 3 * j + 2, col, row)

    def g_end(m):
        landed(outs[m].at[:, :, other], as_rs.at[m])

    steps = dict(
        far=p1_far, early=p1_early, late=p1_late, end=p1_end, first2=p2_first, late2=p2_late, end2=p2_end,
        gram_send=gram_send, gram_sum=gram_sum, update=update, g_start=g_start, g_first=g_first, g_far=g_far,
        g_pass=g_pass, g_last=g_last, g_end=g_end,
    )
    for name, *at in STEPS:
        steps[name](*at)
    for copy in sends:
        copy.wait_send()


def call(nz, width, *args):
    f32, bf16 = jnp.float32, jnp.bfloat16
    dma = pltpu.SemaphoreType.DMA
    vmem = pl.BlockSpec(memory_space=pltpu.VMEM)
    hbm = pl.BlockSpec(memory_space=pl.ANY)
    out = pltpu.VMEM((NX, NY, NC, BLK, width), bf16)
    new = pltpu.VMEM((BLK, width), f32)
    group = BLK // nz
    return pl.pallas_call(
        functools.partial(kernel, nz, width),
        out_shape=(new, new, out, out),
        in_specs=[hbm] * 6,
        out_specs=(vmem,) * 4,
        scratch_shapes=[
            pltpu.VMEM((4, 4, 4, HALF, width), bf16),
            pltpu.VMEM((4, 4, 4, HALF, width), bf16),
            pltpu.VMEM((4, 2, 4, QUART, width), WIRE),
            pltpu.VMEM((4, 2, 4, QUART, width), WIRE),
            pltpu.VMEM((4, 2, 2, 4, QUART, width), WIRE),
            pltpu.VMEM((4, 2, 2, 4, QUART, width), WIRE),
            pltpu.VMEM((4, 4, HALF, width), f32),
            pltpu.VMEM((4, 2, QUART, width), f32),
            pltpu.VMEM((4, 2, 2, QUART, width), f32),
            pltpu.VMEM((2, BLK, width), f32),
            pltpu.VMEM((2, BLK, width), f32),
            pltpu.VMEM((2, BLK, width), f32),
            pltpu.VMEM((2, nz, group, BLK), f32),
            pltpu.VMEM((2, nz - 1, group, BLK), f32),
            pltpu.VMEM((2, nz, group, BLK), f32),
            dma((2, 2)), dma((4, 4)), dma((4, 4)), dma((4, 4)),
            dma((4, 2, 3)), dma((4, 2, 3)), dma((4, 2, 3)), dma((4, 2, 3)),
            dma((2, nz - 1)), dma((2,)), dma((2, nz - 1)), dma((2,)),
            dma((4, 4)), dma((4, 4)), dma((4, 4, 4)), dma((4, 4, 4)), dma((4, 16)), dma((2,)),
        ],
        compiler_params=pltpu.CompilerParams(
            collective_id=0, has_side_effects=True, vmem_limit_bytes=44 * 1024 * 1024
        ),
    )(*args)


def store_kernel(*refs):
    sem = refs[-1]
    copies = [pltpu.make_async_copy(refs[k], refs[4 + k], sem.at[k]) for k in range(4)]
    for copy in copies:
        copy.start()
    for copy in copies:
        copy.wait()


def store(*held):
    return pl.pallas_call(
        store_kernel,
        out_shape=tuple(jax.ShapeDtypeStruct(h.shape, h.dtype) for h in held),
        in_specs=[pl.BlockSpec(memory_space=pltpu.VMEM)] * 4,
        out_specs=(pl.BlockSpec(memory_space=pl.ANY),) * 4,
        scratch_shapes=[pltpu.SemaphoreType.DMA((4,))],
        compiler_params=pltpu.CompilerParams(vmem_limit_bytes=1024 * 1024),
    )(*held)


def body(grad_down, grad_out, momentum_down, momentum_out, master_down, master_out):
    nz = lax.axis_size("mp")
    width = grad_down.shape[-1]
    shape = (NX, NY, NC, BLK, width)
    new_down, new_out, out_down, out_out = store(*call(
        nz, width, grad_down.reshape(shape), grad_out.reshape(shape),
        momentum_down, momentum_out, master_down, master_out,
    ))
    rows = NX * NY * NC * BLK
    return (new_down, new_out, out_down.reshape(rows, width), out_out.reshape(rows, width))


def solution(mesh):
    placed = (
        P("dp", None, "mp"),
        P("dp", None, "mp"),
        P("dp", "mp"),
        P("dp", "mp"),
        P("dp", "mp"),
        P("dp", "mp"),
    )
    return jax.shard_map(
        body,
        mesh=mesh,
        in_specs=placed,
        out_specs=(P("dp", "mp"), P("dp", "mp"), P(None, "mp"), P(None, "mp")),
        check_vma=False,
    )
```

```python
import functools
import math

import jax
import jax.numpy as jnp
from jax import lax
from jax.experimental import pallas as pl
from jax.experimental.pallas import tpu as pltpu
from jax.sharding import PartitionSpec as P

D = 5120
BLK = 128
ITERS = 3
NX, NY, NC = 4, 4, 2
HALF = 64
TOP = 6.0
QUART = 32
MESH = pl.DeviceIdType.MESH

momentum_coef = 0.95
learn_rate = 0.5
decay_rate = 0.1
coef_a = 3.4445
coef_b = -4.775
coef_c = 2.0315
norm_eps = 1e-07

WIRE = jnp.bfloat16
POWER = 12
LOW, HIGH = 2.0**-10.4, 2.0**10.4


def encode(x, bound):
    v = jnp.abs(x) * ((HIGH - LOW) / bound) + LOW
    v = v * v * v
    v = v * v
    v = v * v
    return jnp.where(x < 0, -v, v).astype(WIRE)


def decode(y, bound):
    w = y.astype(jnp.float32)
    v = jnp.exp2(jnp.log(jnp.abs(w)) * (1.0 / (POWER * math.log(2.0))))
    v = (v - LOW) * (bound / (HIGH - LOW))
    return jnp.where(w < 0, -v, v)


STEPS = (
    ("far", 0, 0),
    ("far", 0, 1),
    ("early", 0, 1),
    ("early", 0, 0),
    ("late", 0, 0),
    ("late", 0, 1),
    ("far", 1, 0),
    ("end_early", 0, 1),
    ("far", 1, 1),
    ("end_early", 0, 0),
    ("end_late", 0, 0),
    ("far2", 0, 0),
    ("early2", 0, 0),
    ("end_late", 0, 1),
    ("far2", 0, 1),
    ("early2", 0, 1),
    ("early", 1, 1),
    ("early", 1, 0),
    ("late2", 0, 1),
    ("late2", 0, 0),
    ("late", 1, 1),
    ("late", 1, 0),
    ("end_early", 1, 0),
    ("end2", 0, 0),
    ("end2", 0, 1),
    ("gram_send", 0),
    ("end_early", 1, 1),
    ("end_late", 1, 1),
    ("far2", 1, 1),
    ("end_late", 1, 0),
    ("far2", 1, 0),
    ("early2", 1, 0),
    ("gram_sum", 0),
    ("early2", 1, 1),
    ("late2", 1, 1),
    ("late2", 1, 0),
    ("end2", 1, 1),
    ("upd0", 0),
    ("end2", 1, 0),
    ("gram_send", 1),
    ("upd1", 0),
    ("upd2", 0),
    ("g_own", 0, 1),
    ("g_own", 0, 0),
    ("g_fan", 0, 1, 0),
    ("g_fan", 0, 0, 0),
    ("gram_sum", 1),
    ("g_near", 0, 1),
    ("g_near", 0, 0),
    ("g_fan", 0, 0, 1),
    ("g_fan", 0, 1, 1),
    ("g_pass", 0, 0, 0),
    ("g_fan", 0, 0, 2),
    ("g_fan", 0, 1, 2),
    ("g_fan", 0, 0, 3),
    ("g_pass", 0, 1, 0),
    ("g_fan", 0, 1, 3),
    ("upd0", 1),
    ("upd1", 1),
    ("upd2", 1),
    ("g_own", 1, 0),
    ("g_own", 1, 1),
    ("g_fan", 1, 0, 0),
    ("g_pass", 0, 1, 1),
    ("g_last", 0, 1, 0),
    ("g_pass", 0, 0, 2),
    ("g_fan", 1, 1, 0),
    ("g_near", 1, 1),
    ("g_near", 1, 0),
    ("g_fan", 1, 0, 2),
    ("g_fan", 1, 1, 1),
    ("g_fan", 1, 0, 1),
    ("g_fan", 1, 1, 2),
    ("g_pass", 0, 1, 2),
    ("g_fan", 1, 0, 3),
    ("g_pass", 0, 0, 3),
    ("g_fan", 1, 1, 3),
    ("g_pass", 0, 1, 3),
    ("g_pass", 0, 0, 1),
    ("g_pass", 1, 0, 1),
    ("g_pass", 1, 1, 0),
    ("g_pass", 1, 1, 2),
    ("g_pass", 1, 0, 0),
    ("g_pass", 1, 0, 3),
    ("g_last", 0, 1, 1),
    ("g_pass", 1, 0, 2),
    ("g_last", 0, 0, 0),
    ("g_pass", 1, 1, 1),
    ("g_pass", 1, 1, 3),
    ("g_last", 0, 0, 2),
    ("g_last", 1, 0, 1),
    ("g_last", 1, 1, 2),
    ("g_last", 0, 1, 3),
    ("g_last", 0, 1, 2),
    ("g_last", 1, 0, 0),
    ("g_last", 1, 1, 0),
    ("g_last", 0, 0, 3),
    ("g_last", 0, 0, 1),
    ("g_last", 1, 1, 1),
    ("g_last", 1, 0, 3),
    ("g_last", 1, 0, 2),
    ("g_last", 1, 1, 3),
    ("g_end", 1),
    ("g_end", 0),
)


def dot(a, b):
    return jnp.dot(a, b, precision=lax.Precision.HIGHEST, preferred_element_type=jnp.float32)


def kernel(
    nz, width,
    grad_down, grad_out, mom_down, mom_out, mas_down, mas_out,
    new_down, new_out, out_down, out_out,
    own, sib, s2, r2, s1, r1, acc, t2, rr2, t1, rr1, whole, power, mom, mas, look, gpart, gslot, gfull,
    small_sem, own_sem, sib_ss, sib_rs,
    p1_ss, p1_rs, p2_ss, p2_rs,
    ga_ss, ga_rs, gb_ss, gb_rs,
    aa_ss, aa_rs, ab_ss, ab_rs, as_ss, as_rs,
):
    grads, moms, mass = (grad_down, grad_out), (mom_down, mom_out), (mas_down, mas_out)
    news, outs = (new_down, new_out), (out_down, out_out)
    dp, z = lax.axis_index("dp"), lax.axis_index("mp")
    c = lax.rem(dp, 2)
    chip = lax.div(dp, 2)
    y = lax.rem(chip, NY)
    x = lax.div(chip, NY)
    other = 1 - c

    def wrap(v):
        return lax.rem(v + 4, 4)

    def device(px, py, pc=c, pz=z):
        return ((px * NY + py) * NC + pc, pz)

    sibling = device(x, y, other)
    pos = ((x, y), (y, x))

    def along(h, axis, step):
        use_x = (axis == 0) == (h == 0)
        return device(wrap(x + step), y) if use_x else device(x, wrap(y + step))

    def chip_at(h, a, b):
        return (a, b) if h == 0 else (b, a)

    def remote(src, dst, ss, rs, dev):
        return pltpu.make_async_remote_copy(
            src_ref=src, dst_ref=dst, send_sem=ss, recv_sem=rs, device_id=dev, device_id_type=MESH
        )

    sends = []

    def send(src, dst, ss, rs, dev):
        copy = remote(src, dst, ss, rs, dev)
        copy.start()
        sends.append(copy)

    def landed(dst, rs):
        pltpu.make_async_copy(dst, dst, rs).wait()

    order = (2, 1, 3, 0)

    def source(m, h, da, core):
        a = wrap(pos[h][0] + da)
        if h == 0:
            return grads[m].at[a, :, core, 0:HALF, :]
        return grads[m].at[:, a, core, HALF:BLK, :]

    own_copies = {}
    for m in range(2):
        for da in order:
            for h in range(2):
                mh = 2 * m + h
                copy = pltpu.make_async_copy(source(m, h, da, c), own.at[mh, da], own_sem.at[mh, da])
                copy.start()
                own_copies[mh, da] = copy
    small = []
    for m in range(2):
        for k, (src, dst) in enumerate(((moms[m], mom.at[m]), (mass[m], mas.at[m]))):
            copy = pltpu.make_async_copy(src, dst, small_sem.at[m, k])
            copy.start()
            small.append(copy)

    barrier = pltpu.get_barrier_semaphore()
    peers = [sibling]
    for h in range(2):
        peers += [along(h, 0, 1), along(h, 0, -1)]
    peers += [device(x, y, c, lax.rem(z + k, nz)) for k in range(1, nz)]
    for peer in peers:
        pl.semaphore_signal(barrier, inc=1, device_id=peer, device_id_type=MESH)
    pl.semaphore_wait(barrier, len(peers))

    for m in range(2):
        for da in order:
            for h in range(2):
                mh = 2 * m + h
                send(source(m, h, da, other), sib.at[mh, da], sib_ss.at[mh, da], sib_rs.at[mh, da], sibling)

    def have(m, h, da):
        own_copies[2 * m + h, da].wait()
        landed(sib.at[2 * m + h, da], sib_rs.at[2 * m + h, da])

    def pair(mh, da, b, lo):
        rows = pl.ds(lo, QUART)
        return own[mh, da, b, rows, :].astype(jnp.float32) + sib[mh, da, b, rows, :].astype(jnp.float32)

    def far(m, h):
        have(m, h, 2)
        mh = 2 * m + h
        for d in range(2):
            @pl.loop(0, 4)
            def _(b):
                s2[mh, d, b] = encode(pair(mh, 2, b, QUART * d), 2 * TOP)
            send(s2.at[mh, d], r2.at[mh, d], p1_ss.at[mh, d, 0], p1_rs.at[mh, d, 0], along(h, 0, 1 - 2 * d))

    def early(m, h):
        mh = 2 * m + h
        for d in range(2):
            have(m, h, 1 + 2 * d)

            @pl.loop(0, 4)
            def _(b):
                s1[mh, d, 0, b] = encode(pair(mh, 1 + 2 * d, b, QUART * (1 - d)), 2 * TOP)
            send(s1.at[mh, d, 0], r1.at[mh, d, 0], p1_ss.at[mh, d, 1], p1_rs.at[mh, d, 1], along(h, 0, 1 - 2 * d))

    def late(m, h):
        mh = 2 * m + h
        for d in range(2):
            landed(r2.at[mh, d], p1_rs.at[mh, d, 0])

            @pl.loop(0, 4)
            def _(b):
                s1[mh, d, 1, b] = encode(
                    pair(mh, 1 + 2 * d, b, QUART * d) + decode(r2[mh, d, b], 2 * TOP), 4 * TOP
                )
            send(s1.at[mh, d, 1], r1.at[mh, d, 1], p1_ss.at[mh, d, 2], p1_rs.at[mh, d, 2], along(h, 0, 1 - 2 * d))

    def end_early(m, h):
        have(m, h, 0)
        mh = 2 * m + h
        for d in range(2):
            landed(r1.at[mh, d, 0], p1_rs.at[mh, d, 1])

        @pl.loop(0, 4)
        def _(b):
            for q in range(2):
                acc[mh, b, pl.ds(QUART * q, QUART), :] = (
                    pair(mh, 0, b, QUART * q) + decode(r1[mh, 1 - q, 0, b], 2 * TOP)
                )

    def end_late(m, h):
        mh = 2 * m + h
        for d in range(2):
            landed(r1.at[mh, d, 1], p1_rs.at[mh, d, 2])

        @pl.loop(0, 4)
        def _(b):
            for q in range(2):
                rows = pl.ds(QUART * q, QUART)
                acc[mh, b, rows, :] = acc[mh, b, rows, :] + decode(r1[mh, q, 1, b], 4 * TOP)

    def far2(m, h):
        mh, at = 2 * m + h, pos[h][1]
        for d in range(2):
            t2[mh, d] = encode(acc[mh, wrap(at + 2), pl.ds(QUART * d, QUART), :], 8 * TOP)
            send(t2.at[mh, d], rr2.at[mh, d], p2_ss.at[mh, d, 0], p2_rs.at[mh, d, 0], along(h, 1, 1 - 2 * d))

    def early2(m, h):
        mh, at = 2 * m + h, pos[h][1]
        for d in range(2):
            near = acc[mh, wrap(at + 1 - 2 * d), pl.ds(QUART * (1 - d), QUART), :]
            t1[mh, d, 0] = encode(near, 8 * TOP)
            send(t1.at[mh, d, 0], rr1.at[mh, d, 0], p2_ss.at[mh, d, 1], p2_rs.at[mh, d, 1], along(h, 1, 1 - 2 * d))

    def late2(m, h):
        mh = 2 * m + h
        for d in range(2):
            landed(rr2.at[mh, d], p2_rs.at[mh, d, 0])
            near = acc[mh, wrap(pos[h][1] + 1 - 2 * d), pl.ds(QUART * d, QUART), :]
            t1[mh, d, 1] = encode(near + decode(rr2[mh, d], 8 * TOP), 16 * TOP)
            send(t1.at[mh, d, 1], rr1.at[mh, d, 1], p2_ss.at[mh, d, 2], p2_rs.at[mh, d, 2], along(h, 1, 1 - 2 * d))

    def end2(m, h):
        if m == 0 and h == 0:
            for copy in small:
                copy.wait()
        mh = 2 * m + h
        for d in range(2):
            for e in range(2):
                landed(rr1.at[mh, d, e], p2_rs.at[mh, d, 1 + e])
        for q in range(2):
            rows = pl.ds(HALF * h + QUART * q, QUART)
            total = (
                acc[mh, pos[h][1], pl.ds(QUART * q, QUART), :]
                + decode(rr1[mh, q, 1], 16 * TOP) + decode(rr1[mh, 1 - q, 0], 8 * TOP)
            )
            new = momentum_coef * mom[m, rows, :] + total
            news[m][rows, :] = new
            look[m, rows, :] = total + momentum_coef * new

    def gram_send(m):
        u = look[m]
        gram = lax.dot_general(
            u, u, (((1,), (1,)), ((), ())),
            precision=lax.Precision.HIGHEST, preferred_element_type=jnp.float32,
        )
        gpart[m] = gram.reshape(nz, BLK // nz, BLK)
        for k in range(1, nz):
            to = lax.rem(z + k, nz)
            send(gpart.at[m, to], gslot.at[m, k - 1], ga_ss.at[m, k - 1], ga_rs.at[m], device(x, y, c, to))

    def gram_sum(m):
        landed(gslot.at[m], ga_rs.at[m])
        total = gpart[m, z]
        for k in range(nz - 1):
            total = total + gslot[m, k]
        gfull[m, z] = total
        for k in range(1, nz):
            to = lax.rem(z + k, nz)
            send(gfull.at[m, z], gfull.at[m, z], gb_ss.at[m, k - 1], gb_rs.at[m], device(x, y, c, to))

    def upd0(m):
        landed(gslot.at[m], gb_rs.at[m])
        gram = gfull[m].reshape(BLK, BLK)
        eye = lax.broadcasted_iota(jnp.int32, (BLK, BLK), 0) == lax.broadcasted_iota(jnp.int32, (BLK, BLK), 1)
        diag = jnp.where(eye, gram, 0.0)
        square = jnp.sum(jnp.sum(diag, axis=1, keepdims=True), axis=0, keepdims=True)
        inv = 1.0 / (jnp.sqrt(square) + norm_eps)
        gram = gram * inv * inv
        factor = jnp.where(eye, coef_a, 0.0) + coef_b * gram + coef_c * dot(gram, gram)
        whole[m] = factor * inv
        power[m] = dot(dot(factor, gram), factor)

    def factor_of(gram):
        eye = lax.broadcasted_iota(jnp.int32, (BLK, BLK), 0) == lax.broadcasted_iota(jnp.int32, (BLK, BLK), 1)
        return jnp.where(eye, coef_a, 0.0) + coef_b * gram + coef_c * dot(gram, gram)

    def upd1(m):
        gram = power[m]
        factor = factor_of(gram)
        whole[m] = dot(factor, whole[m])
        power[m] = dot(dot(factor, gram), factor)

    def upd2(m):
        ortho = dot(dot(factor_of(power[m]), whole[m]), look[m])
        scale = learn_rate * 0.2 * math.sqrt(D)
        weights = (1.0 - learn_rate * decay_rate) * mas[m] - scale * ortho
        outs[m][x, y, c] = weights.astype(jnp.bfloat16)

    def block(m, h, a, b, lo=0, n=HALF):
        px, py = chip_at(h, a, b)
        return outs[m].at[px, py, c, pl.ds(HALF * h + lo, n), :]

    def hand(m, h, k, a, b):
        ref = block(m, h, a, b)
        send(ref, ref, as_ss.at[2 * m + h, k], as_rs.at[m], sibling)

    def fan(m, h, j, a):
        mh, ref = 2 * m + h, block(m, h, a, pos[h][1])
        for d in range(2):
            send(ref, ref, ab_ss.at[mh, j, d], ab_rs.at[mh, j, d], along(h, 1, 1 - 2 * d))

    def cols(h):
        a = pos[h][0]
        return (a, wrap(a - 1), wrap(a + 1), wrap(a + 2))

    def g_own(m, h):
        ref = block(m, h, *pos[h])
        for d in range(2):
            send(ref, ref, aa_ss.at[2 * m + h, d], aa_rs.at[2 * m + h, d], along(h, 0, 1 - 2 * d))

    def g_near(m, h):
        mh, b = 2 * m + h, pos[h][1]
        for d in range(2):
            col = cols(h)[1 + d]
            landed(block(m, h, col, b), aa_rs.at[mh, d])
            part = block(m, h, col, b, QUART * d, QUART)
            send(part, part, aa_ss.at[mh, 2 + d], aa_rs.at[mh, 2 + d], along(h, 0, 1 - 2 * d))

    def g_fan(m, h, j):
        mh, b = 2 * m + h, pos[h][1]
        col = cols(h)[j]
        if j == 3:
            for d in range(2):
                landed(block(m, h, col, b, QUART * d, QUART), aa_rs.at[mh, 2 + d])
        fan(m, h, j, col)
        hand(m, h, j, col, b)

    def g_pass(m, h, j):
        mh, b = 2 * m + h, pos[h][1]
        col = cols(h)[j]
        for d in range(2):
            row = wrap(b - 1 + 2 * d)
            landed(block(m, h, col, row), ab_rs.at[mh, j, d])
            part = block(m, h, col, row, QUART * d, QUART)
            send(part, part, ab_ss.at[mh, j, 2 + d], ab_rs.at[mh, j, 2 + d], along(h, 1, 1 - 2 * d))
            hand(m, h, 4 + 3 * j + d, col, row)

    def g_last(m, h, j):
        mh, b = 2 * m + h, pos[h][1]
        col, row = cols(h)[j], wrap(b + 2)
        for d in range(2):
            landed(block(m, h, col, row, QUART * d, QUART), ab_rs.at[mh, j, 2 + d])
        hand(m, h, 4 + 3 * j + 2, col, row)

    def g_end(m):
        landed(outs[m].at[:, :, other], as_rs.at[m])

    steps = dict(
        far=far, early=early, late=late, end_early=end_early, end_late=end_late,
        far2=far2, early2=early2, late2=late2, end2=end2,
        gram_send=gram_send, gram_sum=gram_sum, upd0=upd0, upd1=upd1, upd2=upd2,
        g_own=g_own, g_near=g_near, g_fan=g_fan, g_pass=g_pass, g_last=g_last, g_end=g_end,
    )
    for name, *at in STEPS:
        steps[name](*at)
    for copy in sends:
        copy.wait_send()


def call(nz, width, *args):
    f32, bf16 = jnp.float32, jnp.bfloat16
    dma = pltpu.SemaphoreType.DMA
    vmem = pl.BlockSpec(memory_space=pltpu.VMEM)
    hbm = pl.BlockSpec(memory_space=pl.ANY)
    out = pltpu.VMEM((NX, NY, NC, BLK, width), bf16)
    new = pltpu.VMEM((BLK, width), f32)
    group = BLK // nz
    return pl.pallas_call(
        functools.partial(kernel, nz, width),
        out_shape=(new, new, out, out),
        in_specs=[hbm] * 6,
        out_specs=(vmem,) * 4,
        scratch_shapes=[
            pltpu.VMEM((4, 4, 4, HALF, width), bf16),
            pltpu.VMEM((4, 4, 4, HALF, width), bf16),
            pltpu.VMEM((4, 2, 4, QUART, width), WIRE),
            pltpu.VMEM((4, 2, 4, QUART, width), WIRE),
            pltpu.VMEM((4, 2, 2, 4, QUART, width), WIRE),
            pltpu.VMEM((4, 2, 2, 4, QUART, width), WIRE),
            pltpu.VMEM((4, 4, HALF, width), f32),
            pltpu.VMEM((4, 2, QUART, width), WIRE),
            pltpu.VMEM((4, 2, QUART, width), WIRE),
            pltpu.VMEM((4, 2, 2, QUART, width), WIRE),
            pltpu.VMEM((4, 2, 2, QUART, width), WIRE),
            pltpu.VMEM((2, BLK, BLK), f32),
            pltpu.VMEM((2, BLK, BLK), f32),
            pltpu.VMEM((2, BLK, width), f32),
            pltpu.VMEM((2, BLK, width), f32),
            pltpu.VMEM((2, BLK, width), f32),
            pltpu.VMEM((2, nz, group, BLK), f32),
            pltpu.VMEM((2, nz - 1, group, BLK), f32),
            pltpu.VMEM((2, nz, group, BLK), f32),
            dma((2, 2)), dma((4, 4)), dma((4, 4)), dma((4, 4)),
            dma((4, 2, 3)), dma((4, 2, 3)), dma((4, 2, 3)), dma((4, 2, 3)),
            dma((2, nz - 1)), dma((2,)), dma((2, nz - 1)), dma((2,)),
            dma((4, 4)), dma((4, 4)), dma((4, 4, 4)), dma((4, 4, 4)), dma((4, 16)), dma((2,)),
        ],
        compiler_params=pltpu.CompilerParams(
            collective_id=0, has_side_effects=True, vmem_limit_bytes=44 * 1024 * 1024
        ),
    )(*args)


def store_kernel(*refs):
    sem = refs[-1]
    copies = [pltpu.make_async_copy(refs[k], refs[4 + k], sem.at[k]) for k in range(2)]
    for k in range(2, 4):
        for i in range(NX):
            copies.append(pltpu.make_async_copy(refs[k].at[i], refs[4 + k].at[i], sem.at[NX * (k - 1) + i]))
    for copy in copies:
        copy.start()
    for copy in copies:
        copy.wait()


def store(*held):
    return pl.pallas_call(
        store_kernel,
        out_shape=tuple(jax.ShapeDtypeStruct(h.shape, h.dtype) for h in held),
        in_specs=[pl.BlockSpec(memory_space=pltpu.VMEM)] * 4,
        out_specs=(pl.BlockSpec(memory_space=pl.ANY),) * 4,
        scratch_shapes=[pltpu.SemaphoreType.DMA((3 * NX,))],
        compiler_params=pltpu.CompilerParams(vmem_limit_bytes=1024 * 1024),
    )(*held)


def body(grad_down, grad_out, momentum_down, momentum_out, master_down, master_out):
    nz = lax.axis_size("mp")
    width = grad_down.shape[-1]
    shape = (NX, NY, NC, BLK, width)
    new_down, new_out, out_down, out_out = store(*call(
        nz, width, grad_down.reshape(shape), grad_out.reshape(shape),
        momentum_down, momentum_out, master_down, master_out,
    ))
    rows = NX * NY * NC * BLK
    return (new_down, new_out, out_down.reshape(rows, width), out_out.reshape(rows, width))


def solution(mesh):
    placed = (
        P("dp", None, "mp"),
        P("dp", None, "mp"),
        P("dp", "mp"),
        P("dp", "mp"),
        P("dp", "mp"),
        P("dp", "mp"),
    )
    return jax.shard_map(
        body,
        mesh=mesh,
        in_specs=placed,
        out_specs=(P("dp", "mp"), P("dp", "mp"), P(None, "mp"), P(None, "mp")),
        check_vma=False,
    )
```

```python
import functools
import math

import jax
import jax.numpy as jnp
from jax import lax
from jax.experimental import pallas as pl
from jax.experimental.pallas import tpu as pltpu
from jax.sharding import PartitionSpec as P

D = 5120
BLK = 128
ITERS = 3
NX, NY, NC = 4, 4, 2
HALF = 64
TOP = 6.0
QUART = 32
SPLIT = 2
MESH = pl.DeviceIdType.MESH

momentum_coef = 0.95
learn_rate = 0.5
decay_rate = 0.1
coef_a = 3.4445
coef_b = -4.775
coef_c = 2.0315
norm_eps = 1e-07

WIRE = jnp.bfloat16
POWER = 12
LOW, HIGH = 2.0**-10.4, 2.0**10.4


def encode(x, bound):
    v = jnp.abs(x) * ((HIGH - LOW) / bound) + LOW
    v = v * v * v
    v = v * v
    v = v * v
    return jnp.where(x < 0, -v, v).astype(WIRE)


def decode(y, bound):
    w = y.astype(jnp.float32)
    v = jnp.exp2(jnp.log(jnp.abs(w)) * (1.0 / (POWER * math.log(2.0))))
    v = (v - LOW) * (bound / (HIGH - LOW))
    return jnp.where(w < 0, -v, v)


STEPS = (
    ("far", 0, 0, 0),
    ("far", 0, 1, 0),
    ("far", 0, 0, 1),
    ("far", 0, 1, 1),
    ("early", 0, 0, 0),
    ("early", 0, 1, 0),
    ("late", 0, 0, 0),
    ("late", 0, 1, 0),
    ("early", 0, 0, 1),
    ("late", 0, 0, 1),
    ("early", 0, 1, 1),
    ("late", 0, 1, 1),
    ("end_early", 0, 0, 0),
    ("end_late", 0, 0, 0),
    ("far2", 0, 0),
    ("end_early", 0, 1, 0),
    ("end_late", 0, 1, 0),
    ("far2", 0, 1),
    ("far", 1, 1, 0),
    ("far", 1, 0, 0),
    ("end_early", 0, 0, 1),
    ("end_early", 0, 1, 1),
    ("end_late", 0, 0, 1),
    ("early2", 0, 0),
    ("end_late", 0, 1, 1),
    ("early2", 0, 1),
    ("late2", 0, 0),
    ("late2", 0, 1),
    ("early", 1, 1, 0),
    ("far", 1, 0, 1),
    ("early", 1, 0, 0),
    ("late", 1, 0, 0),
    ("far", 1, 1, 1),
    ("late", 1, 1, 0),
    ("end2", 0, 0),
    ("end2", 0, 1),
    ("gram_send", 0),
    ("early", 1, 1, 1),
    ("early", 1, 0, 1),
    ("late", 1, 1, 1),
    ("end_early", 1, 0, 0),
    ("late", 1, 0, 1),
    ("end_early", 1, 1, 0),
    ("end_late", 1, 0, 0),
    ("far2", 1, 0),
    ("gram_sum", 0),
    ("end_late", 1, 1, 0),
    ("far2", 1, 1),
    ("end_early", 1, 1, 1),
    ("end_late", 1, 1, 1),
    ("end_early", 1, 0, 1),
    ("end_late", 1, 0, 1),
    ("early2", 1, 1),
    ("early2", 1, 0),
    ("late2", 1, 0),
    ("late2", 1, 1),
    ("upd0", 0),
    ("upd1", 0),
    ("upd2", 0),
    ("g_own", 0, 1),
    ("g_own", 0, 0),
    ("end2", 1, 0),
    ("end2", 1, 1),
    ("gram_send", 1),
    ("g_fan", 0, 1, 0),
    ("g_fan", 0, 0, 0),
    ("g_near", 0, 1),
    ("g_near", 0, 0),
    ("g_fan", 0, 0, 2),
    ("g_fan", 0, 1, 2),
    ("g_fan", 0, 1, 1),
    ("g_fan", 0, 0, 1),
    ("gram_sum", 1),
    ("g_pass", 0, 1, 2),
    ("g_pass", 0, 0, 2),
    ("g_pass", 0, 0, 0),
    ("g_fan", 0, 1, 3),
    ("g_pass", 0, 1, 0),
    ("g_fan", 0, 0, 3),
    ("g_pass", 0, 0, 1),
    ("g_pass", 0, 1, 1),
    ("upd0", 1),
    ("upd1", 1),
    ("upd2", 1),
    ("g_own", 1, 0),
    ("g_own", 1, 1),
    ("g_fan", 1, 1, 0),
    ("g_pass", 0, 1, 3),
    ("g_fan", 1, 0, 0),
    ("g_pass", 0, 0, 3),
    ("g_last", 0, 0, 1),
    ("g_near", 1, 0),
    ("g_near", 1, 1),
    ("g_fan", 1, 1, 2),
    ("g_fan", 1, 1, 1),
    ("g_fan", 1, 0, 1),
    ("g_fan", 1, 0, 2),
    ("g_fan", 1, 0, 3),
    ("g_last", 0, 1, 2),
    ("g_last", 0, 1, 3),
    ("g_fan", 1, 1, 3),
    ("g_pass", 1, 0, 1),
    ("g_pass", 1, 1, 0),
    ("g_last", 0, 0, 0),
    ("g_last", 0, 1, 0),
    ("g_pass", 1, 1, 2),
    ("g_pass", 1, 0, 0),
    ("g_pass", 1, 0, 2),
    ("g_pass", 1, 1, 1),
    ("g_pass", 1, 1, 3),
    ("g_pass", 1, 0, 3),
    ("g_last", 1, 0, 1),
    ("g_last", 1, 1, 0),
    ("g_last", 0, 1, 1),
    ("g_last", 1, 0, 0),
    ("g_last", 0, 0, 3),
    ("g_last", 0, 0, 2),
    ("g_last", 1, 1, 1),
    ("g_last", 1, 1, 2),
    ("g_last", 1, 0, 2),
    ("g_end", 0),
    ("g_last", 1, 1, 3),
    ("g_last", 1, 0, 3),
    ("g_end", 1),
)


def dot(a, b):
    return jnp.dot(a, b, precision=lax.Precision.HIGHEST, preferred_element_type=jnp.float32)


def kernel(
    nz, width,
    grad_down, grad_out, mom_down, mom_out, mas_down, mas_out,
    new_down, new_out, out_down, out_out,
    own, sib, s2, r2, s1, r1, acc, t2, rr2, t1, rr1, whole, power, mom, mas, look, gpart, gslot, gfull,
    small_sem, own_sem, sib_ss, sib_rs,
    p1_ss, p1_rs, p2_ss, p2_rs,
    ga_ss, ga_rs, gb_ss, gb_rs,
    aa_ss, aa_rs, ab_ss, ab_rs, as_ss, as_rs,
):
    grads, moms, mass = (grad_down, grad_out), (mom_down, mom_out), (mas_down, mas_out)
    news, outs = (new_down, new_out), (out_down, out_out)
    dp, z = lax.axis_index("dp"), lax.axis_index("mp")
    c = lax.rem(dp, 2)
    chip = lax.div(dp, 2)
    y = lax.rem(chip, NY)
    x = lax.div(chip, NY)
    other = 1 - c

    def wrap(v):
        return lax.rem(v + 4, 4)

    def device(px, py, pc=c, pz=z):
        return ((px * NY + py) * NC + pc, pz)

    sibling = device(x, y, other)
    pos = ((x, y), (y, x))

    def along(h, axis, step):
        use_x = (axis == 0) == (h == 0)
        return device(wrap(x + step), y) if use_x else device(x, wrap(y + step))

    def chip_at(h, a, b):
        return (a, b) if h == 0 else (b, a)

    def remote(src, dst, ss, rs, dev):
        return pltpu.make_async_remote_copy(
            src_ref=src, dst_ref=dst, send_sem=ss, recv_sem=rs, device_id=dev, device_id_type=MESH
        )

    sends = []

    def send(src, dst, ss, rs, dev):
        copy = remote(src, dst, ss, rs, dev)
        copy.start()
        sends.append(copy)

    def landed(dst, rs):
        pltpu.make_async_copy(dst, dst, rs).wait()

    order = (2, 1, 3, 0)

    def source(m, h, da, core):
        a = wrap(pos[h][0] + da)
        if h == 0:
            return grads[m].at[a, :, core, 0:HALF, :]
        return grads[m].at[:, a, core, HALF:BLK, :]

    own_copies = {}
    for m in range(2):
        for da in order:
            for h in range(2):
                mh = 2 * m + h
                copy = pltpu.make_async_copy(source(m, h, da, c), own.at[mh, da], own_sem.at[mh, da])
                copy.start()
                own_copies[mh, da] = copy
    small = []
    for m in range(2):
        for k, (src, dst) in enumerate(((moms[m], mom.at[m]), (mass[m], mas.at[m]))):
            copy = pltpu.make_async_copy(src, dst, small_sem.at[m, k])
            copy.start()
            small.append(copy)

    barrier = pltpu.get_barrier_semaphore()
    peers = [sibling]
    for h in range(2):
        peers += [along(h, 0, 1), along(h, 0, -1)]
    peers += [device(x, y, c, lax.rem(z + k, nz)) for k in range(1, nz)]
    for peer in peers:
        pl.semaphore_signal(barrier, inc=1, device_id=peer, device_id_type=MESH)
    pl.semaphore_wait(barrier, len(peers))

    for m in range(2):
        for da in order:
            for h in range(2):
                mh = 2 * m + h
                send(source(m, h, da, other), sib.at[mh, da], sib_ss.at[mh, da], sib_rs.at[mh, da], sibling)

    arrived = set()

    def have(m, h, da):
        if (m, h, da) not in arrived:
            arrived.add((m, h, da))
            own_copies[2 * m + h, da].wait()
            landed(sib.at[2 * m + h, da], sib_rs.at[2 * m + h, da])

    def ahead(h, k, i):
        return wrap(pos[h][1] + (2 - i if k == 0 else 3 * (1 - i)))

    def pair(mh, da, b, rows):
        return own[mh, da, b, rows, :].astype(jnp.float32) + sib[mh, da, b, rows, :].astype(jnp.float32)

    def piece(t, q):
        n = QUART // SPLIT
        at = lax.rem(t, SPLIT) * n
        return (
            lax.div(t, SPLIT), pl.ds(pl.multiple_of(at, n), n), pl.ds(pl.multiple_of(QUART * q + at, n), n)
        )

    def far(m, h, k):
        have(m, h, 2)
        mh = 2 * m + h
        for d in range(2):
            @pl.loop(0, 2 * SPLIT)
            def _(t):
                i, r, rows = piece(t, d)
                s2[mh, d, k, i, r, :] = encode(pair(mh, 2, ahead(h, k, i), rows), 2 * TOP)
            send(
                s2.at[mh, d, k], r2.at[mh, d, k],
                p1_ss.at[mh, d, 0, k], p1_rs.at[mh, d, 0, k], along(h, 0, 1 - 2 * d),
            )

    def early(m, h, k):
        mh = 2 * m + h
        for d in range(2):
            have(m, h, 1 + 2 * d)

            @pl.loop(0, 2 * SPLIT)
            def _(t):
                i, r, rows = piece(t, 1 - d)
                s1[mh, d, 0, k, i, r, :] = encode(pair(mh, 1 + 2 * d, ahead(h, k, i), rows), 2 * TOP)
            send(
                s1.at[mh, d, 0, k], r1.at[mh, d, 0, k],
                p1_ss.at[mh, d, 1, k], p1_rs.at[mh, d, 1, k], along(h, 0, 1 - 2 * d),
            )

    def late(m, h, k):
        mh = 2 * m + h
        for d in range(2):
            have(m, h, 1 + 2 * d)
            landed(r2.at[mh, d, k], p1_rs.at[mh, d, 0, k])

            @pl.loop(0, 2 * SPLIT)
            def _(t):
                i, r, rows = piece(t, d)
                s1[mh, d, 1, k, i, r, :] = encode(
                    pair(mh, 1 + 2 * d, ahead(h, k, i), rows) + decode(r2[mh, d, k, i, r, :], 2 * TOP), 4 * TOP
                )
            send(
                s1.at[mh, d, 1, k], r1.at[mh, d, 1, k],
                p1_ss.at[mh, d, 2, k], p1_rs.at[mh, d, 2, k], along(h, 0, 1 - 2 * d),
            )

    def end_early(m, h, k):
        have(m, h, 0)
        mh = 2 * m + h
        for d in range(2):
            landed(r1.at[mh, d, 0, k], p1_rs.at[mh, d, 1, k])

        @pl.loop(0, 2 * SPLIT)
        def _(t):
            for q in range(2):
                i, r, rows = piece(t, q)
                b = ahead(h, k, i)
                acc[mh, b, rows, :] = pair(mh, 0, b, rows) + decode(r1[mh, 1 - q, 0, k, i, r, :], 2 * TOP)

    def end_late(m, h, k):
        mh = 2 * m + h
        for d in range(2):
            landed(r1.at[mh, d, 1, k], p1_rs.at[mh, d, 2, k])

        @pl.loop(0, 2 * SPLIT)
        def _(t):
            for q in range(2):
                i, r, rows = piece(t, q)
                b = ahead(h, k, i)
                acc[mh, b, rows, :] = acc[mh, b, rows, :] + decode(r1[mh, q, 1, k, i, r, :], 4 * TOP)

    def far2(m, h):
        mh, at = 2 * m + h, pos[h][1]
        for d in range(2):
            t2[mh, d] = encode(acc[mh, wrap(at + 2), pl.ds(QUART * d, QUART), :], 8 * TOP)
            send(t2.at[mh, d], rr2.at[mh, d], p2_ss.at[mh, d, 0], p2_rs.at[mh, d, 0], along(h, 1, 1 - 2 * d))

    def early2(m, h):
        mh, at = 2 * m + h, pos[h][1]
        for d in range(2):
            near = acc[mh, wrap(at + 1 - 2 * d), pl.ds(QUART * (1 - d), QUART), :]
            t1[mh, d, 0] = encode(near, 8 * TOP)
            send(t1.at[mh, d, 0], rr1.at[mh, d, 0], p2_ss.at[mh, d, 1], p2_rs.at[mh, d, 1], along(h, 1, 1 - 2 * d))

    def late2(m, h):
        mh = 2 * m + h
        for d in range(2):
            landed(rr2.at[mh, d], p2_rs.at[mh, d, 0])
            near = acc[mh, wrap(pos[h][1] + 1 - 2 * d), pl.ds(QUART * d, QUART), :]
            t1[mh, d, 1] = encode(near + decode(rr2[mh, d], 8 * TOP), 16 * TOP)
            send(t1.at[mh, d, 1], rr1.at[mh, d, 1], p2_ss.at[mh, d, 2], p2_rs.at[mh, d, 2], along(h, 1, 1 - 2 * d))

    def end2(m, h):
        if m == 0 and h == 0:
            for copy in small:
                copy.wait()
        mh = 2 * m + h
        for d in range(2):
            for e in range(2):
                landed(rr1.at[mh, d, e], p2_rs.at[mh, d, 1 + e])
        for q in range(2):
            rows = pl.ds(HALF * h + QUART * q, QUART)
            total = (
                acc[mh, pos[h][1], pl.ds(QUART * q, QUART), :]
                + decode(rr1[mh, q, 1], 16 * TOP) + decode(rr1[mh, 1 - q, 0], 8 * TOP)
            )
            new = momentum_coef * mom[m, rows, :] + total
            news[m][rows, :] = new
            look[m, rows, :] = total + momentum_coef * new

    def gram_send(m):
        u = look[m]
        gram = lax.dot_general(
            u, u, (((1,), (1,)), ((), ())),
            precision=lax.Precision.HIGHEST, preferred_element_type=jnp.float32,
        )
        gpart[m] = gram.reshape(nz, BLK // nz, BLK)
        for k in range(1, nz):
            to = lax.rem(z + k, nz)
            send(gpart.at[m, to], gslot.at[m, k - 1], ga_ss.at[m, k - 1], ga_rs.at[m], device(x, y, c, to))

    def gram_sum(m):
        landed(gslot.at[m], ga_rs.at[m])
        total = gpart[m, z]
        for k in range(nz - 1):
            total = total + gslot[m, k]
        gfull[m, z] = total
        for k in range(1, nz):
            to = lax.rem(z + k, nz)
            send(gfull.at[m, z], gfull.at[m, z], gb_ss.at[m, k - 1], gb_rs.at[m], device(x, y, c, to))

    def upd0(m):
        landed(gslot.at[m], gb_rs.at[m])
        gram = gfull[m].reshape(BLK, BLK)
        eye = lax.broadcasted_iota(jnp.int32, (BLK, BLK), 0) == lax.broadcasted_iota(jnp.int32, (BLK, BLK), 1)
        diag = jnp.where(eye, gram, 0.0)
        square = jnp.sum(jnp.sum(diag, axis=1, keepdims=True), axis=0, keepdims=True)
        inv = 1.0 / (jnp.sqrt(square) + norm_eps)
        gram = gram * inv * inv
        factor = jnp.where(eye, coef_a, 0.0) + coef_b * gram + coef_c * dot(gram, gram)
        whole[m] = factor * inv
        power[m] = dot(dot(factor, gram), factor)

    def factor_of(gram):
        eye = lax.broadcasted_iota(jnp.int32, (BLK, BLK), 0) == lax.broadcasted_iota(jnp.int32, (BLK, BLK), 1)
        return jnp.where(eye, coef_a, 0.0) + coef_b * gram + coef_c * dot(gram, gram)

    def upd1(m):
        gram = power[m]
        factor = factor_of(gram)
        whole[m] = dot(factor, whole[m])
        power[m] = dot(dot(factor, gram), factor)

    def upd2(m):
        ortho = dot(dot(factor_of(power[m]), whole[m]), look[m])
        scale = learn_rate * 0.2 * math.sqrt(D)
        weights = (1.0 - learn_rate * decay_rate) * mas[m] - scale * ortho
        outs[m][x, y, c] = weights.astype(jnp.bfloat16)

    def block(m, h, a, b, lo=0, n=HALF):
        px, py = chip_at(h, a, b)
        return outs[m].at[px, py, c, pl.ds(HALF * h + lo, n), :]

    def hand(m, h, k, a, b):
        ref = block(m, h, a, b)
        send(ref, ref, as_ss.at[2 * m + h, k], as_rs.at[m], sibling)

    def fan(m, h, j, a):
        mh, ref = 2 * m + h, block(m, h, a, pos[h][1])
        for d in range(2):
            send(ref, ref, ab_ss.at[mh, j, d], ab_rs.at[mh, j, d], along(h, 1, 1 - 2 * d))

    def cols(h):
        a = pos[h][0]
        return (a, wrap(a - 1), wrap(a + 1), wrap(a + 2))

    def g_own(m, h):
        ref = block(m, h, *pos[h])
        for d in range(2):
            send(ref, ref, aa_ss.at[2 * m + h, d], aa_rs.at[2 * m + h, d], along(h, 0, 1 - 2 * d))

    def g_near(m, h):
        mh, b = 2 * m + h, pos[h][1]
        for d in range(2):
            col = cols(h)[1 + d]
            landed(block(m, h, col, b), aa_rs.at[mh, d])
            part = block(m, h, col, b, QUART * d, QUART)
            send(part, part, aa_ss.at[mh, 2 + d], aa_rs.at[mh, 2 + d], along(h, 0, 1 - 2 * d))

    def g_fan(m, h, j):
        mh, b = 2 * m + h, pos[h][1]
        col = cols(h)[j]
        if j == 3:
            for d in range(2):
                landed(block(m, h, col, b, QUART * d, QUART), aa_rs.at[mh, 2 + d])
        fan(m, h, j, col)
        hand(m, h, j, col, b)

    def g_pass(m, h, j):
        mh, b = 2 * m + h, pos[h][1]
        col = cols(h)[j]
        for d in range(2):
            row = wrap(b - 1 + 2 * d)
            landed(block(m, h, col, row), ab_rs.at[mh, j, d])
            part = block(m, h, col, row, QUART * d, QUART)
            send(part, part, ab_ss.at[mh, j, 2 + d], ab_rs.at[mh, j, 2 + d], along(h, 1, 1 - 2 * d))
            hand(m, h, 4 + 3 * j + d, col, row)

    def g_last(m, h, j):
        mh, b = 2 * m + h, pos[h][1]
        col, row = cols(h)[j], wrap(b + 2)
        for d in range(2):
            landed(block(m, h, col, row, QUART * d, QUART), ab_rs.at[mh, j, 2 + d])
        hand(m, h, 4 + 3 * j + 2, col, row)

    def g_end(m):
        landed(outs[m].at[:, :, other], as_rs.at[m])

    steps = dict(
        far=far, early=early, late=late, end_early=end_early, end_late=end_late,
        far2=far2, early2=early2, late2=late2, end2=end2,
        gram_send=gram_send, gram_sum=gram_sum, upd0=upd0, upd1=upd1, upd2=upd2,
        g_own=g_own, g_near=g_near, g_fan=g_fan, g_pass=g_pass, g_last=g_last, g_end=g_end,
    )
    for name, *at in STEPS:
        steps[name](*at)
    for copy in sends:
        copy.wait_send()


def call(nz, width, *args):
    f32, bf16 = jnp.float32, jnp.bfloat16
    dma = pltpu.SemaphoreType.DMA
    vmem = pl.BlockSpec(memory_space=pltpu.VMEM)
    hbm = pl.BlockSpec(memory_space=pl.ANY)
    out = pltpu.VMEM((NX, NY, NC, BLK, width), bf16)
    new = pltpu.VMEM((BLK, width), f32)
    group = BLK // nz
    return pl.pallas_call(
        functools.partial(kernel, nz, width),
        out_shape=(new, new, out, out),
        in_specs=[hbm] * 6,
        out_specs=(vmem,) * 4,
        scratch_shapes=[
            pltpu.VMEM((4, 4, 4, HALF, width), bf16),
            pltpu.VMEM((4, 4, 4, HALF, width), bf16),
            pltpu.VMEM((4, 2, 2, 2, QUART, width), WIRE),
            pltpu.VMEM((4, 2, 2, 2, QUART, width), WIRE),
            pltpu.VMEM((4, 2, 2, 2, 2, QUART, width), WIRE),
            pltpu.VMEM((4, 2, 2, 2, 2, QUART, width), WIRE),
            pltpu.VMEM((4, 4, HALF, width), f32),
            pltpu.VMEM((4, 2, QUART, width), WIRE),
            pltpu.VMEM((4, 2, QUART, width), WIRE),
            pltpu.VMEM((4, 2, 2, QUART, width), WIRE),
            pltpu.VMEM((4, 2, 2, QUART, width), WIRE),
            pltpu.VMEM((2, BLK, BLK), f32),
            pltpu.VMEM((2, BLK, BLK), f32),
            pltpu.VMEM((2, BLK, width), f32),
            pltpu.VMEM((2, BLK, width), f32),
            pltpu.VMEM((2, BLK, width), f32),
            pltpu.VMEM((2, nz, group, BLK), f32),
            pltpu.VMEM((2, nz - 1, group, BLK), f32),
            pltpu.VMEM((2, nz, group, BLK), f32),
            dma((2, 2)), dma((4, 4)), dma((4, 4)), dma((4, 4)),
            dma((4, 2, 3, 2)), dma((4, 2, 3, 2)), dma((4, 2, 3)), dma((4, 2, 3)),
            dma((2, nz - 1)), dma((2,)), dma((2, nz - 1)), dma((2,)),
            dma((4, 4)), dma((4, 4)), dma((4, 4, 4)), dma((4, 4, 4)), dma((4, 16)), dma((2,)),
        ],
        compiler_params=pltpu.CompilerParams(
            collective_id=0, has_side_effects=True, vmem_limit_bytes=44 * 1024 * 1024
        ),
    )(*args)


def store_kernel(*refs):
    sem = refs[-1]
    copies = [pltpu.make_async_copy(refs[k], refs[4 + k], sem.at[k]) for k in range(2)]
    for k in range(2, 4):
        for i in range(NX):
            copies.append(pltpu.make_async_copy(refs[k].at[i], refs[4 + k].at[i], sem.at[NX * (k - 1) + i]))
    for copy in copies:
        copy.start()
    for copy in copies:
        copy.wait()


def store(*held):
    return pl.pallas_call(
        store_kernel,
        out_shape=tuple(jax.ShapeDtypeStruct(h.shape, h.dtype) for h in held),
        in_specs=[pl.BlockSpec(memory_space=pltpu.VMEM)] * 4,
        out_specs=(pl.BlockSpec(memory_space=pl.ANY),) * 4,
        scratch_shapes=[pltpu.SemaphoreType.DMA((3 * NX,))],
        compiler_params=pltpu.CompilerParams(vmem_limit_bytes=1024 * 1024),
    )(*held)


def body(grad_down, grad_out, momentum_down, momentum_out, master_down, master_out):
    nz = lax.axis_size("mp")
    width = grad_down.shape[-1]
    shape = (NX, NY, NC, BLK, width)
    new_down, new_out, out_down, out_out = store(*call(
        nz, width, grad_down.reshape(shape), grad_out.reshape(shape),
        momentum_down, momentum_out, master_down, master_out,
    ))
    rows = NX * NY * NC * BLK
    return (new_down, new_out, out_down.reshape(rows, width), out_out.reshape(rows, width))


def solution(mesh):
    placed = (
        P("dp", None, "mp"),
        P("dp", None, "mp"),
        P("dp", "mp"),
        P("dp", "mp"),
        P("dp", "mp"),
        P("dp", "mp"),
    )
    return jax.shard_map(
        body,
        mesh=mesh,
        in_specs=placed,
        out_specs=(P("dp", "mp"), P("dp", "mp"), P(None, "mp"), P(None, "mp")),
        check_vma=False,
    )
```

```python
import functools
import math

import jax
import jax.numpy as jnp
from jax import lax
from jax.experimental import pallas as pl
from jax.experimental.pallas import tpu as pltpu
from jax.sharding import PartitionSpec as P

D = 5120
BLK = 128
ITERS = 3
NX, NY, NC = 4, 4, 2
HALF = 64
TOP = 6.0
QUART = 32
SPLIT = 2
MESH = pl.DeviceIdType.MESH

momentum_coef = 0.95
learn_rate = 0.5
decay_rate = 0.1
coef_a = 3.4445
coef_b = -4.775
coef_c = 2.0315
norm_eps = 1e-07

WIRE = jnp.bfloat16
POWER = 12
LOW, HIGH = 2.0**-10.4, 2.0**10.4


def encode(x, bound):
    v = jnp.abs(x) * ((HIGH - LOW) / bound) + LOW
    v = v * v * v
    v = v * v
    v = v * v
    return jnp.where(x < 0, -v, v).astype(WIRE)


def decode(y, bound):
    w = y.astype(jnp.float32)
    v = jnp.exp2(jnp.log(jnp.abs(w)) * (1.0 / (POWER * math.log(2.0))))
    v = (v - LOW) * (bound / (HIGH - LOW))
    return jnp.where(w < 0, -v, v)


STEPS = (
    ("far", 0, 0, 0),
    ("far", 0, 1, 0),
    ("far", 0, 0, 1),
    ("far", 0, 1, 1),
    ("early", 0, 0, 0),
    ("early", 0, 1, 0),
    ("late", 0, 0, 0),
    ("late", 0, 1, 0),
    ("early", 0, 0, 1),
    ("late", 0, 0, 1),
    ("early", 0, 1, 1),
    ("late", 0, 1, 1),
    ("end_early", 0, 0, 0),
    ("end_late", 0, 0, 0),
    ("far2", 0, 0),
    ("end_early", 0, 1, 0),
    ("end_late", 0, 1, 0),
    ("far2", 0, 1),
    ("far", 1, 1, 0),
    ("far", 1, 0, 0),
    ("end_early", 0, 0, 1),
    ("end_early", 0, 1, 1),
    ("end_late", 0, 0, 1),
    ("early2", 0, 0),
    ("end_late", 0, 1, 1),
    ("early2", 0, 1),
    ("late2", 0, 0),
    ("late2", 0, 1),
    ("early", 1, 1, 0),
    ("far", 1, 0, 1),
    ("early", 1, 0, 0),
    ("late", 1, 0, 0),
    ("far", 1, 1, 1),
    ("late", 1, 1, 0),
    ("end2", 0, 0),
    ("end2", 0, 1),
    ("gram_send", 0),
    ("early", 1, 1, 1),
    ("early", 1, 0, 1),
    ("late", 1, 1, 1),
    ("end_early", 1, 0, 0),
    ("late", 1, 0, 1),
    ("end_early", 1, 1, 0),
    ("end_late", 1, 0, 0),
    ("far2", 1, 0),
    ("gram_sum", 0),
    ("end_late", 1, 1, 0),
    ("far2", 1, 1),
    ("end_early", 1, 1, 1),
    ("end_late", 1, 1, 1),
    ("end_early", 1, 0, 1),
    ("end_late", 1, 0, 1),
    ("early2", 1, 1),
    ("early2", 1, 0),
    ("late2", 1, 0),
    ("late2", 1, 1),
    ("upd0", 0),
    ("upd1", 0),
    ("upd2", 0),
    ("g_own", 0, 1),
    ("g_own", 0, 0),
    ("end2", 1, 0),
    ("end2", 1, 1),
    ("gram_send", 1),
    ("g_fan", 0, 1, 0),
    ("g_fan", 0, 0, 0),
    ("g_near", 0, 1),
    ("g_near", 0, 0),
    ("g_fan", 0, 0, 2),
    ("g_fan", 0, 1, 2),
    ("g_fan", 0, 1, 1),
    ("g_fan", 0, 0, 1),
    ("gram_sum", 1),
    ("g_pass", 0, 1, 2),
    ("g_pass", 0, 0, 2),
    ("g_pass", 0, 0, 0),
    ("g_fan", 0, 1, 3),
    ("g_pass", 0, 1, 0),
    ("g_fan", 0, 0, 3),
    ("g_pass", 0, 0, 1),
    ("g_pass", 0, 1, 1),
    ("upd0", 1),
    ("upd1", 1),
    ("upd2", 1),
    ("g_own", 1, 0),
    ("g_own", 1, 1),
    ("g_fan", 1, 1, 0),
    ("g_pass", 0, 1, 3),
    ("g_fan", 1, 0, 0),
    ("g_pass", 0, 0, 3),
    ("g_last", 0, 0, 1),
    ("g_near", 1, 0),
    ("g_near", 1, 1),
    ("g_fan", 1, 1, 2),
    ("g_fan", 1, 1, 1),
    ("g_fan", 1, 0, 1),
    ("g_fan", 1, 0, 2),
    ("g_fan", 1, 0, 3),
    ("g_last", 0, 1, 2),
    ("g_last", 0, 1, 3),
    ("g_fan", 1, 1, 3),
    ("g_pass", 1, 0, 1),
    ("g_pass", 1, 1, 0),
    ("g_last", 0, 0, 0),
    ("g_last", 0, 1, 0),
    ("g_pass", 1, 1, 2),
    ("g_pass", 1, 0, 0),
    ("g_pass", 1, 0, 2),
    ("g_pass", 1, 1, 1),
    ("g_pass", 1, 1, 3),
    ("g_pass", 1, 0, 3),
    ("g_last", 1, 0, 1),
    ("g_last", 1, 1, 0),
    ("g_last", 0, 1, 1),
    ("g_last", 1, 0, 0),
    ("g_last", 0, 0, 3),
    ("g_last", 0, 0, 2),
    ("g_last", 1, 1, 1),
    ("g_last", 1, 1, 2),
    ("g_last", 1, 0, 2),
    ("g_end", 0),
    ("g_last", 1, 1, 3),
    ("g_last", 1, 0, 3),
    ("g_end", 1),
)


def dot(a, b):
    return jnp.dot(a, b, precision=lax.Precision.HIGHEST, preferred_element_type=jnp.float32)


def kernel(
    nz, width,
    grad_down, grad_out, mom_down, mom_out, mas_down, mas_out,
    new_down, new_out, out_down, out_out,
    own, sib, s2, r2, s1, r1, acc, t2, rr2, t1, rr1, whole, power, mom, mas, look, gpart, gslot, gfull,
    small_sem, own_sem, sib_ss, sib_rs,
    p1_ss, p1_rs, p2_ss, p2_rs,
    ga_ss, ga_rs, gb_ss, gb_rs,
    aa_ss, aa_rs, ab_ss, ab_rs, as_ss, as_rs,
):
    grads, moms, mass = (grad_down, grad_out), (mom_down, mom_out), (mas_down, mas_out)
    news, outs = (new_down, new_out), (out_down, out_out)
    dp, z = lax.axis_index("dp"), lax.axis_index("mp")
    c = lax.rem(dp, 2)
    chip = lax.div(dp, 2)
    y = lax.rem(chip, NY)
    x = lax.div(chip, NY)
    other = 1 - c

    def wrap(v):
        return lax.rem(v + 4, 4)

    def device(px, py, pc=c, pz=z):
        return ((px * NY + py) * NC + pc, pz)

    sibling = device(x, y, other)
    pos = ((x, y), (y, x))

    def along(h, axis, step):
        use_x = (axis == 0) == (h == 0)
        return device(wrap(x + step), y) if use_x else device(x, wrap(y + step))

    def chip_at(h, a, b):
        return (a, b) if h == 0 else (b, a)

    def remote(src, dst, ss, rs, dev):
        return pltpu.make_async_remote_copy(
            src_ref=src, dst_ref=dst, send_sem=ss, recv_sem=rs, device_id=dev, device_id_type=MESH
        )

    def send(src, dst, ss, rs, dev):
        remote(src, dst, ss, rs, dev).start()

    def landed(dst, rs):
        pltpu.make_async_copy(dst, dst, rs).wait()

    order = (2, 1, 3, 0)

    def source(m, h, da, core):
        a = wrap(pos[h][0] + da)
        if h == 0:
            return grads[m].at[a, :, core, 0:HALF, :]
        return grads[m].at[:, a, core, HALF:BLK, :]

    own_copies = {}
    for m in range(2):
        for da in order:
            for h in range(2):
                mh = 2 * m + h
                copy = pltpu.make_async_copy(source(m, h, da, c), own.at[mh, da], own_sem.at[mh, da])
                copy.start()
                own_copies[mh, da] = copy
    small = []
    for m in range(2):
        for k, (src, dst) in enumerate(((moms[m], mom.at[m]), (mass[m], mas.at[m]))):
            copy = pltpu.make_async_copy(src, dst, small_sem.at[m, k])
            copy.start()
            small.append(copy)

    barrier = pltpu.get_barrier_semaphore()
    peers = [sibling]
    for h in range(2):
        peers += [along(h, 0, 1), along(h, 0, -1)]
    peers += [device(x, y, c, lax.rem(z + k, nz)) for k in range(1, nz)]
    for peer in peers:
        pl.semaphore_signal(barrier, inc=1, device_id=peer, device_id_type=MESH)
    pl.semaphore_wait(barrier, len(peers))

    for m in range(2):
        for da in order:
            for h in range(2):
                mh = 2 * m + h
                send(source(m, h, da, other), sib.at[mh, da], sib_ss.at[0], sib_rs.at[mh, da], sibling)

    arrived = set()

    def have(m, h, da):
        if (m, h, da) not in arrived:
            arrived.add((m, h, da))
            own_copies[2 * m + h, da].wait()
            landed(sib.at[2 * m + h, da], sib_rs.at[2 * m + h, da])

    def ahead(h, k, i):
        return wrap(pos[h][1] + (2 - i if k == 0 else 3 * (1 - i)))

    def pair(mh, da, b, rows):
        return own[mh, da, b, rows, :].astype(jnp.float32) + sib[mh, da, b, rows, :].astype(jnp.float32)

    def piece(t, q):
        n = QUART // SPLIT
        at = lax.rem(t, SPLIT) * n
        return (
            lax.div(t, SPLIT), pl.ds(pl.multiple_of(at, n), n), pl.ds(pl.multiple_of(QUART * q + at, n), n)
        )

    def far(m, h, k):
        have(m, h, 2)
        mh = 2 * m + h
        for d in range(2):
            @pl.loop(0, 2 * SPLIT)
            def _(t):
                i, r, rows = piece(t, d)
                s2[mh, d, k, i, r, :] = encode(pair(mh, 2, ahead(h, k, i), rows), 2 * TOP)
            send(
                s2.at[mh, d, k], r2.at[mh, d, k],
                p1_ss.at[mh, 0], p1_rs.at[mh, d, 0, k], along(h, 0, 1 - 2 * d),
            )

    def early(m, h, k):
        mh = 2 * m + h
        for d in range(2):
            have(m, h, 1 + 2 * d)

            @pl.loop(0, 2 * SPLIT)
            def _(t):
                i, r, rows = piece(t, 1 - d)
                s1[mh, d, 0, k, i, r, :] = encode(pair(mh, 1 + 2 * d, ahead(h, k, i), rows), 2 * TOP)
            send(
                s1.at[mh, d, 0, k], r1.at[mh, d, 0, k],
                p1_ss.at[mh, 1], p1_rs.at[mh, d, 1, k], along(h, 0, 1 - 2 * d),
            )

    def late(m, h, k):
        mh = 2 * m + h
        for d in range(2):
            have(m, h, 1 + 2 * d)
            landed(r2.at[mh, d, k], p1_rs.at[mh, d, 0, k])

            @pl.loop(0, 2 * SPLIT)
            def _(t):
                i, r, rows = piece(t, d)
                s1[mh, d, 1, k, i, r, :] = encode(
                    pair(mh, 1 + 2 * d, ahead(h, k, i), rows) + decode(r2[mh, d, k, i, r, :], 2 * TOP), 4 * TOP
                )
            send(
                s1.at[mh, d, 1, k], r1.at[mh, d, 1, k],
                p1_ss.at[mh, 1], p1_rs.at[mh, d, 2, k], along(h, 0, 1 - 2 * d),
            )

    def end_early(m, h, k):
        have(m, h, 0)
        mh = 2 * m + h
        for d in range(2):
            landed(r1.at[mh, d, 0, k], p1_rs.at[mh, d, 1, k])

        @pl.loop(0, 2 * SPLIT)
        def _(t):
            for q in range(2):
                i, r, rows = piece(t, q)
                b = ahead(h, k, i)
                acc[mh, b, rows, :] = pair(mh, 0, b, rows) + decode(r1[mh, 1 - q, 0, k, i, r, :], 2 * TOP)

    def end_late(m, h, k):
        mh = 2 * m + h
        for d in range(2):
            landed(r1.at[mh, d, 1, k], p1_rs.at[mh, d, 2, k])

        @pl.loop(0, 2 * SPLIT)
        def _(t):
            for q in range(2):
                i, r, rows = piece(t, q)
                b = ahead(h, k, i)
                acc[mh, b, rows, :] = acc[mh, b, rows, :] + decode(r1[mh, q, 1, k, i, r, :], 4 * TOP)

    def far2(m, h):
        mh, at = 2 * m + h, pos[h][1]
        for d in range(2):
            t2[mh, d] = encode(acc[mh, wrap(at + 2), pl.ds(QUART * d, QUART), :], 8 * TOP)
            send(t2.at[mh, d], rr2.at[mh, d], p2_ss.at[mh, 0], p2_rs.at[mh, d, 0], along(h, 1, 1 - 2 * d))

    def early2(m, h):
        mh, at = 2 * m + h, pos[h][1]
        for d in range(2):
            near = acc[mh, wrap(at + 1 - 2 * d), pl.ds(QUART * (1 - d), QUART), :]
            t1[mh, d, 0] = encode(near, 8 * TOP)
            send(t1.at[mh, d, 0], rr1.at[mh, d, 0], p2_ss.at[mh, 1], p2_rs.at[mh, d, 1], along(h, 1, 1 - 2 * d))

    def late2(m, h):
        mh = 2 * m + h
        for d in range(2):
            landed(rr2.at[mh, d], p2_rs.at[mh, d, 0])
            near = acc[mh, wrap(pos[h][1] + 1 - 2 * d), pl.ds(QUART * d, QUART), :]
            t1[mh, d, 1] = encode(near + decode(rr2[mh, d], 8 * TOP), 16 * TOP)
            send(t1.at[mh, d, 1], rr1.at[mh, d, 1], p2_ss.at[mh, 1], p2_rs.at[mh, d, 2], along(h, 1, 1 - 2 * d))

    def end2(m, h):
        if m == 0 and h == 0:
            for copy in small:
                copy.wait()
        mh = 2 * m + h
        for d in range(2):
            for e in range(2):
                landed(rr1.at[mh, d, e], p2_rs.at[mh, d, 1 + e])
        for q in range(2):
            rows = pl.ds(HALF * h + QUART * q, QUART)
            total = (
                acc[mh, pos[h][1], pl.ds(QUART * q, QUART), :]
                + decode(rr1[mh, q, 1], 16 * TOP) + decode(rr1[mh, 1 - q, 0], 8 * TOP)
            )
            new = momentum_coef * mom[m, rows, :] + total
            news[m][rows, :] = new
            look[m, rows, :] = total + momentum_coef * new

    def gram_send(m):
        u = look[m]
        gram = lax.dot_general(
            u, u, (((1,), (1,)), ((), ())),
            precision=lax.Precision.HIGHEST, preferred_element_type=jnp.float32,
        )
        gpart[m] = gram.reshape(nz, BLK // nz, BLK)
        for k in range(1, nz):
            to = lax.rem(z + k, nz)
            send(gpart.at[m, to], gslot.at[m, k - 1], ga_ss.at[m], ga_rs.at[m], device(x, y, c, to))

    def gram_sum(m):
        landed(gslot.at[m], ga_rs.at[m])
        total = gpart[m, z]
        for k in range(nz - 1):
            total = total + gslot[m, k]
        gfull[m, z] = total
        for k in range(1, nz):
            to = lax.rem(z + k, nz)
            send(gfull.at[m, z], gfull.at[m, z], gb_ss.at[m], gb_rs.at[m], device(x, y, c, to))

    def upd0(m):
        landed(gslot.at[m], gb_rs.at[m])
        gram = gfull[m].reshape(BLK, BLK)
        eye = lax.broadcasted_iota(jnp.int32, (BLK, BLK), 0) == lax.broadcasted_iota(jnp.int32, (BLK, BLK), 1)
        diag = jnp.where(eye, gram, 0.0)
        square = jnp.sum(jnp.sum(diag, axis=1, keepdims=True), axis=0, keepdims=True)
        inv = 1.0 / (jnp.sqrt(square) + norm_eps)
        gram = gram * inv * inv
        factor = jnp.where(eye, coef_a, 0.0) + coef_b * gram + coef_c * dot(gram, gram)
        whole[m] = factor * inv
        power[m] = dot(dot(factor, gram), factor)

    def factor_of(gram):
        eye = lax.broadcasted_iota(jnp.int32, (BLK, BLK), 0) == lax.broadcasted_iota(jnp.int32, (BLK, BLK), 1)
        return jnp.where(eye, coef_a, 0.0) + coef_b * gram + coef_c * dot(gram, gram)

    def upd1(m):
        gram = power[m]
        factor = factor_of(gram)
        whole[m] = dot(factor, whole[m])
        power[m] = dot(dot(factor, gram), factor)

    def upd2(m):
        ortho = dot(dot(factor_of(power[m]), whole[m]), look[m])
        scale = learn_rate * 0.2 * math.sqrt(D)
        weights = (1.0 - learn_rate * decay_rate) * mas[m] - scale * ortho
        outs[m][x, y, c] = weights.astype(jnp.bfloat16)

    def block(m, h, a, b, lo=0, n=HALF):
        px, py = chip_at(h, a, b)
        return outs[m].at[px, py, c, pl.ds(HALF * h + lo, n), :]

    def hand(m, h, k, a, b):
        ref = block(m, h, a, b)
        send(ref, ref, as_ss.at[m], as_rs.at[m], sibling)

    def fan(m, h, j, a):
        mh, ref = 2 * m + h, block(m, h, a, pos[h][1])
        for d in range(2):
            send(ref, ref, ab_ss.at[mh], ab_rs.at[mh, j, d], along(h, 1, 1 - 2 * d))

    def cols(h):
        a = pos[h][0]
        return (a, wrap(a - 1), wrap(a + 1), wrap(a + 2))

    def g_own(m, h):
        ref = block(m, h, *pos[h])
        for d in range(2):
            send(ref, ref, aa_ss.at[2 * m + h], aa_rs.at[2 * m + h, d], along(h, 0, 1 - 2 * d))

    def g_near(m, h):
        mh, b = 2 * m + h, pos[h][1]
        for d in range(2):
            col = cols(h)[1 + d]
            landed(block(m, h, col, b), aa_rs.at[mh, d])
            part = block(m, h, col, b, QUART * d, QUART)
            send(part, part, aa_ss.at[mh], aa_rs.at[mh, 2 + d], along(h, 0, 1 - 2 * d))

    def g_fan(m, h, j):
        mh, b = 2 * m + h, pos[h][1]
        col = cols(h)[j]
        if j == 3:
            for d in range(2):
                landed(block(m, h, col, b, QUART * d, QUART), aa_rs.at[mh, 2 + d])
        fan(m, h, j, col)
        hand(m, h, j, col, b)

    def g_pass(m, h, j):
        mh, b = 2 * m + h, pos[h][1]
        col = cols(h)[j]
        for d in range(2):
            row = wrap(b - 1 + 2 * d)
            landed(block(m, h, col, row), ab_rs.at[mh, j, d])
            part = block(m, h, col, row, QUART * d, QUART)
            send(part, part, ab_ss.at[mh], ab_rs.at[mh, j, 2 + d], along(h, 1, 1 - 2 * d))
            hand(m, h, 4 + 3 * j + d, col, row)

    def g_last(m, h, j):
        mh, b = 2 * m + h, pos[h][1]
        col, row = cols(h)[j], wrap(b + 2)
        for d in range(2):
            landed(block(m, h, col, row, QUART * d, QUART), ab_rs.at[mh, j, 2 + d])
        hand(m, h, 4 + 3 * j + 2, col, row)

    def g_end(m):
        landed(outs[m].at[:, :, other], as_rs.at[m])

    steps = dict(
        far=far, early=early, late=late, end_early=end_early, end_late=end_late,
        far2=far2, early2=early2, late2=late2, end2=end2,
        gram_send=gram_send, gram_sum=gram_sum, upd0=upd0, upd1=upd1, upd2=upd2,
        g_own=g_own, g_near=g_near, g_fan=g_fan, g_pass=g_pass, g_last=g_last, g_end=g_end,
    )
    for name, *at in STEPS:
        steps[name](*at)
    landed(sib, sib_ss.at[0])
    for mh in range(4):
        landed(s2.at[mh], p1_ss.at[mh, 0])
        landed(s1.at[mh], p1_ss.at[mh, 1])
        landed(t2.at[mh], p2_ss.at[mh, 0])
        landed(t1.at[mh], p2_ss.at[mh, 1])
        landed(own.at[0, 0, pl.ds(0, 3)], aa_ss.at[mh])
        landed(own.at[0, pl.ds(0, 3)], ab_ss.at[mh])
    for m in range(2):
        landed(gslot.at[m], ga_ss.at[m])
        landed(gslot.at[m], gb_ss.at[m])
        landed(outs[m].at[:, :, c], as_ss.at[m])


def call(nz, width, *args):
    f32, bf16 = jnp.float32, jnp.bfloat16
    dma = pltpu.SemaphoreType.DMA
    vmem = pl.BlockSpec(memory_space=pltpu.VMEM)
    hbm = pl.BlockSpec(memory_space=pl.ANY)
    out = pltpu.VMEM((NX, NY, NC, BLK, width), bf16)
    new = pltpu.VMEM((BLK, width), f32)
    group = BLK // nz
    return pl.pallas_call(
        functools.partial(kernel, nz, width),
        out_shape=(new, new, out, out),
        in_specs=[hbm] * 6,
        out_specs=(vmem,) * 4,
        scratch_shapes=[
            pltpu.VMEM((4, 4, 4, HALF, width), bf16),
            pltpu.VMEM((4, 4, 4, HALF, width), bf16),
            pltpu.VMEM((4, 2, 2, 2, QUART, width), WIRE),
            pltpu.VMEM((4, 2, 2, 2, QUART, width), WIRE),
            pltpu.VMEM((4, 2, 2, 2, 2, QUART, width), WIRE),
            pltpu.VMEM((4, 2, 2, 2, 2, QUART, width), WIRE),
            pltpu.VMEM((4, 4, HALF, width), f32),
            pltpu.VMEM((4, 2, QUART, width), WIRE),
            pltpu.VMEM((4, 2, QUART, width), WIRE),
            pltpu.VMEM((4, 2, 2, QUART, width), WIRE),
            pltpu.VMEM((4, 2, 2, QUART, width), WIRE),
            pltpu.VMEM((2, BLK, BLK), f32),
            pltpu.VMEM((2, BLK, BLK), f32),
            pltpu.VMEM((2, BLK, width), f32),
            pltpu.VMEM((2, BLK, width), f32),
            pltpu.VMEM((2, BLK, width), f32),
            pltpu.VMEM((2, nz, group, BLK), f32),
            pltpu.VMEM((2, nz - 1, group, BLK), f32),
            pltpu.VMEM((2, nz, group, BLK), f32),
            dma((2, 2)), dma((4, 4)), dma((1,)), dma((4, 4)),
            dma((4, 2)), dma((4, 2, 3, 2)), dma((4, 2)), dma((4, 2, 3)),
            dma((2,)), dma((2,)), dma((2,)), dma((2,)),
            dma((4,)), dma((4, 4)), dma((4,)), dma((4, 4, 4)), dma((2,)), dma((2,)),
        ],
        compiler_params=pltpu.CompilerParams(
            collective_id=0, has_side_effects=True, vmem_limit_bytes=44 * 1024 * 1024
        ),
    )(*args)


def store_kernel(*refs):
    sem = refs[-1]
    copies = [pltpu.make_async_copy(refs[k], refs[4 + k], sem.at[k]) for k in range(2)]
    for k in range(2, 4):
        for i in range(NX):
            copies.append(pltpu.make_async_copy(refs[k].at[i], refs[4 + k].at[i], sem.at[NX * (k - 1) + i]))
    for copy in copies:
        copy.start()
    for copy in copies:
        copy.wait()


def store(*held):
    return pl.pallas_call(
        store_kernel,
        out_shape=tuple(jax.ShapeDtypeStruct(h.shape, h.dtype) for h in held),
        in_specs=[pl.BlockSpec(memory_space=pltpu.VMEM)] * 4,
        out_specs=(pl.BlockSpec(memory_space=pl.ANY),) * 4,
        scratch_shapes=[pltpu.SemaphoreType.DMA((3 * NX,))],
        compiler_params=pltpu.CompilerParams(vmem_limit_bytes=1024 * 1024),
    )(*held)


def body(grad_down, grad_out, momentum_down, momentum_out, master_down, master_out):
    nz = lax.axis_size("mp")
    width = grad_down.shape[-1]
    shape = (NX, NY, NC, BLK, width)
    new_down, new_out, out_down, out_out = store(*call(
        nz, width, grad_down.reshape(shape), grad_out.reshape(shape),
        momentum_down, momentum_out, master_down, master_out,
    ))
    rows = NX * NY * NC * BLK
    return (new_down, new_out, out_down.reshape(rows, width), out_out.reshape(rows, width))


def solution(mesh):
    placed = (
        P("dp", None, "mp"),
        P("dp", None, "mp"),
        P("dp", "mp"),
        P("dp", "mp"),
        P("dp", "mp"),
        P("dp", "mp"),
    )
    return jax.shard_map(
        body,
        mesh=mesh,
        in_specs=placed,
        out_specs=(P("dp", "mp"), P("dp", "mp"), P(None, "mp"), P(None, "mp")),
        check_vma=False,
    )
```

```python
import functools
import math

import jax
import jax.numpy as jnp
from jax import lax
from jax.experimental import pallas as pl
from jax.experimental.pallas import tpu as pltpu
from jax.sharding import PartitionSpec as P

D = 5120
BLK = 128
ITERS = 3
NX, NY, NC = 4, 4, 2
HALF = 64
TOP = 6.0
QUART = 32
SPLIT = 2
MESH = pl.DeviceIdType.MESH

momentum_coef = 0.95
learn_rate = 0.5
decay_rate = 0.1
coef_a = 3.4445
coef_b = -4.775
coef_c = 2.0315
norm_eps = 1e-07

WIRE = jnp.bfloat16
POWER = 12
LOW, HIGH = 2.0**-10.4, 2.0**10.4


def encode(x, bound):
    v = jnp.abs(x) * ((HIGH - LOW) / bound) + LOW
    v = v * v * v
    v = v * v
    v = v * v
    return jnp.where(x < 0, -v, v).astype(WIRE)


def decode(y, bound):
    w = y.astype(jnp.float32)
    v = jnp.exp2(jnp.log(jnp.abs(w)) * (1.0 / (POWER * math.log(2.0))))
    v = (v - LOW) * (bound / (HIGH - LOW))
    return jnp.where(w < 0, -v, v)


STEPS = (
    ("far", 0, 0, 0),
    ("far", 0, 1, 0),
    ("far", 0, 1, 1),
    ("far", 0, 0, 1),
    ("early", 0, 0, 0),
    ("early", 0, 1, 0),
    ("late", 0, 0, 0),
    ("late", 0, 1, 0),
    ("early", 0, 0, 1),
    ("early", 0, 1, 1),
    ("late", 0, 0, 1),
    ("end_early", 0, 0, 0),
    ("late", 0, 1, 1),
    ("end_early", 0, 1, 0),
    ("end_late", 0, 0, 0),
    ("end_late", 0, 1, 0),
    ("far2", 0, 0),
    ("far2", 0, 1),
    ("far", 1, 0, 0),
    ("far", 1, 1, 0),
    ("end_early", 0, 1, 1),
    ("end_early", 0, 0, 1),
    ("end_late", 0, 0, 1),
    ("early2", 0, 0),
    ("end_late", 0, 1, 1),
    ("early2", 0, 1),
    ("late2", 0, 0),
    ("late2", 0, 1),
    ("early", 1, 0, 0),
    ("early", 1, 1, 0),
    ("far", 1, 1, 1),
    ("late", 1, 1, 0),
    ("far", 1, 0, 1),
    ("late", 1, 0, 0),
    ("end2", 0, 0),
    ("end2", 0, 1),
    ("gram_send", 0),
    ("early", 1, 1, 1),
    ("early", 1, 0, 1),
    ("late", 1, 1, 1),
    ("end_early", 1, 1, 0),
    ("late", 1, 0, 1),
    ("end_late", 1, 1, 0),
    ("end_early", 1, 0, 0),
    ("end_late", 1, 0, 0),
    ("gram_sum", 0),
    ("far2", 1, 0),
    ("far2", 1, 1),
    ("end_early", 1, 1, 1),
    ("end_late", 1, 1, 1),
    ("early2", 1, 1),
    ("end_early", 1, 0, 1),
    ("end_late", 1, 0, 1),
    ("early2", 1, 0),
    ("late2", 1, 0),
    ("late2", 1, 1),
    ("upd0", 0),
    ("upd1", 0),
    ("upd2", 0),
    ("g_own", 0, 1),
    ("g_own", 0, 0),
    ("end2", 1, 0),
    ("end2", 1, 1),
    ("gram_send", 1),
    ("g_fan", 0, 1, 0),
    ("g_fan", 0, 0, 0),
    ("g_near", 0, 0),
    ("g_near", 0, 1),
    ("g_fan", 0, 1, 1),
    ("g_fan", 0, 0, 2),
    ("g_fan", 0, 1, 2),
    ("g_fan", 0, 0, 1),
    ("gram_sum", 1),
    ("g_fan", 0, 0, 3),
    ("g_fan", 0, 1, 3),
    ("g_pass", 0, 0, 2),
    ("g_pass", 0, 1, 1),
    ("g_pass", 0, 1, 0),
    ("g_pass", 0, 0, 0),
    ("upd0", 1),
    ("g_pass", 0, 1, 2),
    ("g_pass", 0, 0, 1),
    ("upd1", 1),
    ("upd2", 1),
    ("g_own", 1, 0),
    ("g_own", 1, 1),
    ("g_fan", 1, 1, 0),
    ("g_pass", 0, 1, 3),
    ("g_fan", 1, 0, 0),
    ("g_last", 0, 1, 0),
    ("g_last", 0, 0, 1),
    ("g_last", 0, 0, 2),
    ("g_last", 0, 1, 2),
    ("g_pass", 0, 0, 3),
    ("g_near", 1, 0),
    ("g_near", 1, 1),
    ("g_fan", 1, 1, 2),
    ("g_fan", 1, 1, 1),
    ("g_fan", 1, 0, 1),
    ("g_fan", 1, 0, 2),
    ("g_fan", 1, 0, 3),
    ("g_fan", 1, 1, 3),
    ("g_pass", 1, 0, 0),
    ("g_pass", 1, 1, 2),
    ("g_pass", 1, 1, 0),
    ("g_last", 0, 1, 1),
    ("g_last", 0, 0, 3),
    ("g_last", 0, 1, 3),
    ("g_pass", 1, 0, 1),
    ("g_pass", 1, 1, 1),
    ("g_pass", 1, 0, 2),
    ("g_pass", 1, 1, 3),
    ("g_pass", 1, 0, 3),
    ("g_last", 0, 0, 0),
    ("g_last", 1, 0, 1),
    ("g_last", 1, 0, 2),
    ("g_last", 1, 1, 2),
    ("g_last", 1, 0, 0),
    ("g_last", 1, 1, 0),
    ("g_end", 0),
    ("g_last", 1, 1, 1),
    ("g_last", 1, 1, 3),
    ("g_last", 1, 0, 3),
    ("g_end", 1),
)


def dot(a, b):
    return jnp.dot(a, b, precision=lax.Precision.HIGHEST, preferred_element_type=jnp.float32)


def kernel(
    nz, width,
    grad_down, grad_out, mom_down, mom_out, mas_down, mas_out,
    new_down, new_out, out_down, out_out,
    own, sib, s2, r2, s1, r1, acc, t2, rr2, t1, rr1, whole, power, mom, mas, look, gpart, gslot, gfull,
    small_sem, own_sem, sib_ss, sib_rs,
    p1_ss, p1_rs, p2_ss, p2_rs,
    ga_ss, ga_rs, gb_ss, gb_rs,
    aa_ss, aa_rs, ab_ss, ab_rs, as_ss, as_rs,
):
    grads, moms, mass = (grad_down, grad_out), (mom_down, mom_out), (mas_down, mas_out)
    news, outs = (new_down, new_out), (out_down, out_out)
    dp, z = lax.axis_index("dp"), lax.axis_index("mp")
    c = lax.rem(dp, 2)
    chip = lax.div(dp, 2)
    y = lax.rem(chip, NY)
    x = lax.div(chip, NY)
    other = 1 - c

    def wrap(v):
        return lax.rem(v + 4, 4)

    def device(px, py, pc=c, pz=z):
        return ((px * NY + py) * NC + pc, pz)

    sibling = device(x, y, other)
    pos = ((x, y), (y, x))

    def along(h, axis, step):
        use_x = (axis == 0) == (h == 0)
        return device(wrap(x + step), y) if use_x else device(x, wrap(y + step))

    def chip_at(h, a, b):
        return (a, b) if h == 0 else (b, a)

    def remote(src, dst, ss, rs, dev):
        return pltpu.make_async_remote_copy(
            src_ref=src, dst_ref=dst, send_sem=ss, recv_sem=rs, device_id=dev, device_id_type=MESH
        )

    def send(src, dst, ss, rs, dev):
        remote(src, dst, ss, rs, dev).start()

    def landed(dst, rs):
        pltpu.make_async_copy(dst, dst, rs).wait()

    order = (2, 1, 3, 0)

    def source(m, h, da, core):
        a = wrap(pos[h][0] + da)
        if h == 0:
            return grads[m].at[a, :, core, 0:HALF, :]
        return grads[m].at[:, a, core, HALF:BLK, :]

    own_copies = {}
    for m in range(2):
        for da in order:
            for h in range(2):
                mh = 2 * m + h
                copy = pltpu.make_async_copy(source(m, h, da, c), own.at[mh, da], own_sem.at[mh, da])
                copy.start()
                own_copies[mh, da] = copy
    small = []
    for m in range(2):
        for k, (src, dst) in enumerate(((moms[m], mom.at[m]), (mass[m], mas.at[m]))):
            copy = pltpu.make_async_copy(src, dst, small_sem.at[m, k])
            copy.start()
            small.append(copy)

    barrier = pltpu.get_barrier_semaphore()
    peers = [sibling]
    for h in range(2):
        peers += [along(h, 0, 1), along(h, 0, -1)]
    peers += [device(x, y, c, lax.rem(z + k, nz)) for k in range(1, nz)]
    for peer in peers:
        pl.semaphore_signal(barrier, inc=1, device_id=peer, device_id_type=MESH)
    pl.semaphore_wait(barrier, len(peers))

    for m in range(2):
        for da in order:
            for h in range(2):
                mh = 2 * m + h
                send(source(m, h, da, other), sib.at[mh, da], sib_ss.at[0], sib_rs.at[mh, da], sibling)

    arrived = set()

    def have(m, h, da):
        if (m, h, da) not in arrived:
            arrived.add((m, h, da))
            own_copies[2 * m + h, da].wait()
            landed(sib.at[2 * m + h, da], sib_rs.at[2 * m + h, da])

    def ahead(h, k, i):
        return wrap(pos[h][1] + (2 - i if k == 0 else 3 * (1 - i)))

    def pair(mh, da, b, rows):
        return own[mh, da, b, rows, :].astype(jnp.float32) + sib[mh, da, b, rows, :].astype(jnp.float32)

    def piece(t, q):
        n = QUART // SPLIT
        at = lax.rem(t, SPLIT) * n
        return (
            lax.div(t, SPLIT), pl.ds(pl.multiple_of(at, n), n), pl.ds(pl.multiple_of(QUART * q + at, n), n)
        )

    def far(m, h, k):
        have(m, h, 2)
        mh = 2 * m + h
        for d in range(2):
            @pl.loop(0, 2 * SPLIT)
            def _(t):
                i, r, rows = piece(t, d)
                s2[mh, d, k, i, r, :] = encode(pair(mh, 2, ahead(h, k, i), rows), 2 * TOP)
            send(
                s2.at[mh, d, k], r2.at[mh, d, k],
                p1_ss.at[mh, 0], p1_rs.at[mh, d, 0, k], along(h, 0, 1 - 2 * d),
            )

    def early(m, h, k):
        mh = 2 * m + h
        for d in range(2):
            have(m, h, 1 + 2 * d)

            @pl.loop(0, 2 * SPLIT)
            def _(t):
                i, r, rows = piece(t, 1 - d)
                s1[mh, d, 0, k, i, r, :] = encode(pair(mh, 1 + 2 * d, ahead(h, k, i), rows), 2 * TOP)
            send(
                s1.at[mh, d, 0, k], r1.at[mh, d, 0, k],
                p1_ss.at[mh, 1], p1_rs.at[mh, d, 1, k], along(h, 0, 1 - 2 * d),
            )

    def late(m, h, k):
        mh = 2 * m + h
        for d in range(2):
            have(m, h, 1 + 2 * d)
            landed(r2.at[mh, d, k], p1_rs.at[mh, d, 0, k])

            @pl.loop(0, 2 * SPLIT)
            def _(t):
                i, r, rows = piece(t, d)
                s1[mh, d, 1, k, i, r, :] = encode(
                    pair(mh, 1 + 2 * d, ahead(h, k, i), rows) + decode(r2[mh, d, k, i, r, :], 2 * TOP), 4 * TOP
                )
            send(
                s1.at[mh, d, 1, k], r1.at[mh, d, 1, k],
                p1_ss.at[mh, 1], p1_rs.at[mh, d, 2, k], along(h, 0, 1 - 2 * d),
            )

    def end_early(m, h, k):
        have(m, h, 0)
        mh = 2 * m + h
        for d in range(2):
            landed(r1.at[mh, d, 0, k], p1_rs.at[mh, d, 1, k])

        @pl.loop(0, 2 * SPLIT)
        def _(t):
            for q in range(2):
                i, r, rows = piece(t, q)
                b = ahead(h, k, i)
                acc[mh, b, rows, :] = pair(mh, 0, b, rows) + decode(r1[mh, 1 - q, 0, k, i, r, :], 2 * TOP)

    def end_late(m, h, k):
        mh = 2 * m + h
        for d in range(2):
            landed(r1.at[mh, d, 1, k], p1_rs.at[mh, d, 2, k])

        @pl.loop(0, 2 * SPLIT)
        def _(t):
            for q in range(2):
                i, r, rows = piece(t, q)
                b = ahead(h, k, i)
                acc[mh, b, rows, :] = acc[mh, b, rows, :] + decode(r1[mh, q, 1, k, i, r, :], 4 * TOP)

    def far2(m, h):
        mh, at = 2 * m + h, pos[h][1]
        for d in range(2):
            t2[mh, d] = encode(acc[mh, wrap(at + 2), pl.ds(QUART * d, QUART), :], 8 * TOP)
            send(t2.at[mh, d], rr2.at[mh, d], p2_ss.at[mh, 0], p2_rs.at[mh, d, 0], along(h, 1, 1 - 2 * d))

    def early2(m, h):
        mh, at = 2 * m + h, pos[h][1]
        for d in range(2):
            near = acc[mh, wrap(at + 1 - 2 * d), pl.ds(QUART * (1 - d), QUART), :]
            t1[mh, d, 0] = encode(near, 8 * TOP)
            send(t1.at[mh, d, 0], rr1.at[mh, d, 0], p2_ss.at[mh, 1], p2_rs.at[mh, d, 1], along(h, 1, 1 - 2 * d))

    def late2(m, h):
        mh = 2 * m + h
        for d in range(2):
            landed(rr2.at[mh, d], p2_rs.at[mh, d, 0])
            near = acc[mh, wrap(pos[h][1] + 1 - 2 * d), pl.ds(QUART * d, QUART), :]
            t1[mh, d, 1] = encode(near + decode(rr2[mh, d], 8 * TOP), 16 * TOP)
            send(t1.at[mh, d, 1], rr1.at[mh, d, 1], p2_ss.at[mh, 1], p2_rs.at[mh, d, 2], along(h, 1, 1 - 2 * d))

    def end2(m, h):
        if m == 0 and h == 0:
            for copy in small:
                copy.wait()
        mh = 2 * m + h
        for d in range(2):
            for e in range(2):
                landed(rr1.at[mh, d, e], p2_rs.at[mh, d, 1 + e])
        for q in range(2):
            rows = pl.ds(HALF * h + QUART * q, QUART)
            total = (
                acc[mh, pos[h][1], pl.ds(QUART * q, QUART), :]
                + decode(rr1[mh, q, 1], 16 * TOP) + decode(rr1[mh, 1 - q, 0], 8 * TOP)
            )
            new = momentum_coef * mom[m, rows, :] + total
            news[m][rows, :] = new
            look[m, rows, :] = total + momentum_coef * new

    def gram_send(m):
        u = look[m]
        gram = lax.dot_general(
            u, u, (((1,), (1,)), ((), ())),
            precision=lax.Precision.HIGHEST, preferred_element_type=jnp.float32,
        )
        gpart[m] = gram.reshape(nz, BLK // nz, BLK)
        for k in range(1, nz):
            to = lax.rem(z + k, nz)
            send(gpart.at[m, to], gslot.at[m, k - 1], ga_ss.at[m], ga_rs.at[m], device(x, y, c, to))

    def gram_sum(m):
        landed(gslot.at[m], ga_rs.at[m])
        total = gpart[m, z]
        for k in range(nz - 1):
            total = total + gslot[m, k]
        gfull[m, z] = total
        for k in range(1, nz):
            to = lax.rem(z + k, nz)
            send(gfull.at[m, z], gfull.at[m, z], gb_ss.at[m], gb_rs.at[m], device(x, y, c, to))

    def upd0(m):
        landed(gslot.at[m], gb_rs.at[m])
        gram = gfull[m].reshape(BLK, BLK)
        eye = lax.broadcasted_iota(jnp.int32, (BLK, BLK), 0) == lax.broadcasted_iota(jnp.int32, (BLK, BLK), 1)
        diag = jnp.where(eye, gram, 0.0)
        square = jnp.sum(jnp.sum(diag, axis=1, keepdims=True), axis=0, keepdims=True)
        inv = 1.0 / (jnp.sqrt(square) + norm_eps)
        gram = gram * inv * inv
        factor = jnp.where(eye, coef_a, 0.0) + coef_b * gram + coef_c * dot(gram, gram)
        whole[m] = factor * inv
        power[m] = dot(dot(factor, gram), factor)

    def factor_of(gram):
        eye = lax.broadcasted_iota(jnp.int32, (BLK, BLK), 0) == lax.broadcasted_iota(jnp.int32, (BLK, BLK), 1)
        return jnp.where(eye, coef_a, 0.0) + coef_b * gram + coef_c * dot(gram, gram)

    def upd1(m):
        gram = power[m]
        factor = factor_of(gram)
        whole[m] = dot(factor, whole[m])
        power[m] = dot(dot(factor, gram), factor)

    def upd2(m):
        ortho = dot(dot(factor_of(power[m]), whole[m]), look[m])
        scale = learn_rate * 0.2 * math.sqrt(D)
        weights = (1.0 - learn_rate * decay_rate) * mas[m] - scale * ortho
        outs[m][x, y, c] = weights.astype(jnp.bfloat16)

    def block(m, h, a, b, lo=0, n=HALF):
        px, py = chip_at(h, a, b)
        return outs[m].at[px, py, c, pl.ds(HALF * h + lo, n), :]

    def hand(m, h, k, a, b):
        ref = block(m, h, a, b)
        send(ref, ref, as_ss.at[m], as_rs.at[m], sibling)

    def fan(m, h, j, a):
        mh, ref = 2 * m + h, block(m, h, a, pos[h][1])
        for d in range(2):
            send(ref, ref, ab_ss.at[mh], ab_rs.at[mh, j, d], along(h, 1, 1 - 2 * d))

    def cols(h):
        a = pos[h][0]
        return (a, wrap(a - 1), wrap(a + 1), wrap(a + 2))

    def g_own(m, h):
        ref = block(m, h, *pos[h])
        for d in range(2):
            send(ref, ref, aa_ss.at[2 * m + h], aa_rs.at[2 * m + h, d], along(h, 0, 1 - 2 * d))

    def g_near(m, h):
        mh, b = 2 * m + h, pos[h][1]
        for d in range(2):
            col = cols(h)[1 + d]
            landed(block(m, h, col, b), aa_rs.at[mh, d])
            part = block(m, h, col, b, QUART * d, QUART)
            send(part, part, aa_ss.at[mh], aa_rs.at[mh, 2 + d], along(h, 0, 1 - 2 * d))

    def g_fan(m, h, j):
        mh, b = 2 * m + h, pos[h][1]
        col = cols(h)[j]
        if j == 3:
            for d in range(2):
                landed(block(m, h, col, b, QUART * d, QUART), aa_rs.at[mh, 2 + d])
        fan(m, h, j, col)
        hand(m, h, j, col, b)

    def g_pass(m, h, j):
        mh, b = 2 * m + h, pos[h][1]
        col = cols(h)[j]
        for d in range(2):
            row = wrap(b - 1 + 2 * d)
            landed(block(m, h, col, row), ab_rs.at[mh, j, d])
            part = block(m, h, col, row, QUART * d, QUART)
            send(part, part, ab_ss.at[mh], ab_rs.at[mh, j, 2 + d], along(h, 1, 1 - 2 * d))
            hand(m, h, 4 + 3 * j + d, col, row)

    def g_last(m, h, j):
        mh, b = 2 * m + h, pos[h][1]
        col, row = cols(h)[j], wrap(b + 2)
        for d in range(2):
            landed(block(m, h, col, row, QUART * d, QUART), ab_rs.at[mh, j, 2 + d])
        hand(m, h, 4 + 3 * j + 2, col, row)

    def g_end(m):
        landed(outs[m].at[:, :, other], as_rs.at[m])

    steps = dict(
        far=far, early=early, late=late, end_early=end_early, end_late=end_late,
        far2=far2, early2=early2, late2=late2, end2=end2,
        gram_send=gram_send, gram_sum=gram_sum, upd0=upd0, upd1=upd1, upd2=upd2,
        g_own=g_own, g_near=g_near, g_fan=g_fan, g_pass=g_pass, g_last=g_last, g_end=g_end,
    )
    for name, *at in STEPS:
        steps[name](*at)
    landed(sib, sib_ss.at[0])
    for mh in range(4):
        landed(s2.at[mh], p1_ss.at[mh, 0])
        landed(s1.at[mh], p1_ss.at[mh, 1])
        landed(t2.at[mh], p2_ss.at[mh, 0])
        landed(t1.at[mh], p2_ss.at[mh, 1])
        landed(own.at[0, 0, pl.ds(0, 3)], aa_ss.at[mh])
        landed(own.at[0, pl.ds(0, 3)], ab_ss.at[mh])
    for m in range(2):
        landed(gslot.at[m], ga_ss.at[m])
        landed(gslot.at[m], gb_ss.at[m])
        landed(outs[m].at[:, :, c], as_ss.at[m])


def call(nz, width, *args):
    f32, bf16 = jnp.float32, jnp.bfloat16
    dma = pltpu.SemaphoreType.DMA
    vmem = pl.BlockSpec(memory_space=pltpu.VMEM)
    hbm = pl.BlockSpec(memory_space=pl.ANY)
    out = pltpu.VMEM((NX, NY, NC, BLK, width), bf16)
    new = pltpu.VMEM((BLK, width), f32)
    group = BLK // nz
    return pl.pallas_call(
        functools.partial(kernel, nz, width),
        out_shape=(new, new, out, out),
        in_specs=[hbm] * 6,
        out_specs=(vmem,) * 4,
        scratch_shapes=[
            pltpu.VMEM((4, 4, 4, HALF, width), bf16),
            pltpu.VMEM((4, 4, 4, HALF, width), bf16),
            pltpu.VMEM((4, 2, 2, 2, QUART, width), WIRE),
            pltpu.VMEM((4, 2, 2, 2, QUART, width), WIRE),
            pltpu.VMEM((4, 2, 2, 2, 2, QUART, width), WIRE),
            pltpu.VMEM((4, 2, 2, 2, 2, QUART, width), WIRE),
            pltpu.VMEM((4, 4, HALF, width), f32),
            pltpu.VMEM((4, 2, QUART, width), WIRE),
            pltpu.VMEM((4, 2, QUART, width), WIRE),
            pltpu.VMEM((4, 2, 2, QUART, width), WIRE),
            pltpu.VMEM((4, 2, 2, QUART, width), WIRE),
            pltpu.VMEM((2, BLK, BLK), f32),
            pltpu.VMEM((2, BLK, BLK), f32),
            pltpu.VMEM((2, BLK, width), f32),
            pltpu.VMEM((2, BLK, width), f32),
            pltpu.VMEM((2, BLK, width), f32),
            pltpu.VMEM((2, nz, group, BLK), f32),
            pltpu.VMEM((2, nz - 1, group, BLK), f32),
            pltpu.VMEM((2, nz, group, BLK), f32),
            dma((2, 2)), dma((4, 4)), dma((1,)), dma((4, 4)),
            dma((4, 2)), dma((4, 2, 3, 2)), dma((4, 2)), dma((4, 2, 3)),
            dma((2,)), dma((2,)), dma((2,)), dma((2,)),
            dma((4,)), dma((4, 4)), dma((4,)), dma((4, 4, 4)), dma((2,)), dma((2,)),
        ],
        compiler_params=pltpu.CompilerParams(
            collective_id=0, has_side_effects=True, vmem_limit_bytes=44 * 1024 * 1024
        ),
    )(*args)


def store_kernel(*refs):
    sem = refs[-1]
    copies = [pltpu.make_async_copy(refs[k], refs[4 + k], sem.at[k]) for k in range(2)]
    for k in range(2, 4):
        for i in range(NX):
            copies.append(pltpu.make_async_copy(refs[k].at[i], refs[4 + k].at[i], sem.at[NX * (k - 1) + i]))
    for copy in copies:
        copy.start()
    for copy in copies:
        copy.wait()


def store(*held):
    return pl.pallas_call(
        store_kernel,
        out_shape=tuple(jax.ShapeDtypeStruct(h.shape, h.dtype) for h in held),
        in_specs=[pl.BlockSpec(memory_space=pltpu.VMEM)] * 4,
        out_specs=(pl.BlockSpec(memory_space=pl.ANY),) * 4,
        scratch_shapes=[pltpu.SemaphoreType.DMA((3 * NX,))],
        compiler_params=pltpu.CompilerParams(vmem_limit_bytes=1024 * 1024),
    )(*held)


def body(grad_down, grad_out, momentum_down, momentum_out, master_down, master_out):
    nz = lax.axis_size("mp")
    width = grad_down.shape[-1]
    shape = (NX, NY, NC, BLK, width)
    new_down, new_out, out_down, out_out = store(*call(
        nz, width, grad_down.reshape(shape), grad_out.reshape(shape),
        momentum_down, momentum_out, master_down, master_out,
    ))
    rows = NX * NY * NC * BLK
    return (new_down, new_out, out_down.reshape(rows, width), out_out.reshape(rows, width))


def solution(mesh):
    placed = (
        P("dp", None, "mp"),
        P("dp", None, "mp"),
        P("dp", "mp"),
        P("dp", "mp"),
        P("dp", "mp"),
        P("dp", "mp"),
    )
    return jax.shard_map(
        body,
        mesh=mesh,
        in_specs=placed,
        out_specs=(P("dp", "mp"), P("dp", "mp"), P(None, "mp"), P(None, "mp")),
        check_vma=False,
    )
```
